32 devices in a mesh: pts: 4 (over x, core), coord: 8 (over z, y).
Axes of the slice: x: 2, y: 2, z: 4, core: 2. Of those that a mesh axis runs over, the one named last changes fastest.
Arguments:
- point_seed: int32 [256], P('pts'), may hold values from 0 to 16777215
- pert_seed: int32 [256, 16], P('pts'), may hold values from 0 to 16777215
- source_coef: float32 [100000], P('coord'), may hold values from -9 to 9
- w1: bfloat16 [1024, 100000], P(None, 'coord'), may hold values from -0.009765625 to 0.009765625
- b1: float32 [1024], replicated, may hold values from -3 to 3
- w2: bfloat16 [1024, 1024], replicated, may hold values from -0.1875 to 0.1875
- w3: bfloat16 [1024], replicated, may hold values from -0.1875 to 0.1875
Outputs:
- residual: float32 [256], P(('pts', 'coord'))
- grad_w1: bfloat16 [1024, 100000], P('pts', 'coord')
- grad_w2: float32 [1024, 1024], P('coord')
- grad_b1: float32 [1024], P('coord')
- grad_w3: float32 [1024], P('coord')
The draws below stay inside these ranges and needn't reach their ends.
All inputs are finite; a program needn't handle non-finite values.
Results may differ from the reference program's by a relative error of at most 0.023.
Values may be sent and summed in bfloat16 or wider, within the bound.
No kernel may reach another device: no remote copies, remote signals or barrier semaphores. Data moves between devices by JAX's collectives and lax.ppermute only.
A program may use at most 128 MiB of HBM per device.

```python
import math
import jax
import jax.numpy as jnp
from jax import lax

D = 100000
H = 1024
K = 16
PTS_DEV = 64
POINTS = 256
N_PTS = 4


def draw_source_coef(key, part):
    position = jnp.arange(D, dtype=jnp.float32) / (D - 1)
    normal_part = jax.random.truncated_normal(key, -3.0, 3.0, (D,), jnp.float32)
    return normal_part * (1.0 + 2.0 * position)


def place_ends(drawn, own_key, least, high):
    spot = [jax.random.randint(jax.random.fold_in(own_key, axis), (), 0, length) for axis, length in enumerate(drawn.shape)]
    main_axis = drawn.shape.index(max(drawn.shape))
    next_to = spot[:main_axis] + [(spot[main_axis] + 1) % drawn.shape[main_axis]] + spot[main_axis + 1:]
    return drawn.at[tuple(spot)].set(least).at[tuple(next_to)].set(high)


def block_levels(rng, extent, cuts, smallest, largest):
    level, own = 1.0, jax.random.fold_in(rng, 6)
    for dim, blocks in cuts:
        heights = jnp.exp(jax.random.uniform(jax.random.fold_in(own, dim), (blocks,), jnp.float32, smallest / len(cuts), largest / len(cuts)))
        level = level * jnp.repeat(heights, extent[dim] // blocks).reshape([-1 if axis == dim else 1 for axis in range(len(extent))])
    return level


def scatter_about(own_key, extent, width, most, shards=(), kind=jnp.bfloat16):
    drawn = width * jax.random.normal(own_key, extent, jnp.float32)
    if shards:
        drawn = drawn * block_levels(own_key, extent, shards, -0.22, 0.18)
    return jnp.clip(drawn, -most, most).astype(kind)


def setup_inputs(seed: int = 0) -> dict:
    streams_of = jax.random.split(jax.random.key(seed), 8)
    point_seed = place_ends(jax.random.randint(streams_of[0], (POINTS,), 0, 16777216), jax.random.fold_in(streams_of[0], 1), 0, 16777215).astype(jnp.int32)
    pert_seed = place_ends(jax.random.randint(streams_of[1], (POINTS, K), 0, 16777216), jax.random.fold_in(streams_of[1], 1), 0, 16777215).astype(jnp.int32)
    source_coef = draw_source_coef(jax.random.fold_in(streams_of[7], 71), 0)
    w1 = scatter_about(streams_of[3], (H, D), (4 * D) ** -0.5, 0.009765625, ((1, 8),))
    b1 = scatter_about(streams_of[4], (H,), 0.5, 3.0, (), jnp.float32)
    w2 = scatter_about(streams_of[5], (H, H), H ** -0.5, 0.1875)
    w3 = scatter_about(streams_of[6], (H,), H ** -0.5, 0.1875)
    return dict(point_seed=point_seed, pert_seed=pert_seed, source_coef=source_coef, w1=w1, b1=b1, w2=w2, w3=w3)


hash_factor = 73244475
NOISE_SCALE = 2.0
READOUT = 0.0625

def shuffle_bits(packed_bits):
    return packed_bits ^ lax.shift_right_logical(packed_bits, jnp.full_like(packed_bits, 16))

def mix_bits(packed_bits):
    packed_bits = shuffle_bits(packed_bits)
    packed_bits = shuffle_bits(packed_bits * hash_factor)
    return shuffle_bits(packed_bits * hash_factor)

def to_unit(packed_bits):
    return ((packed_bits & 8388607).astype(jnp.float32) + 0.5) * (1.0 / 8388608.0)

def column_keys(columns):
    return (mix_bits(columns * 4), mix_bits(columns * 4 + 1), mix_bits(columns * 4 + 2))

def perturbed_rows(point_seeds, pert_seeds, column_hash, coef_part):
    key_zero, key_one, key_two = column_hash
    count_points, count_samples = pert_seeds.shape
    uniform_point = to_unit(mix_bits(key_two[None, :] ^ point_seeds[:, None]))
    coords = 2.0 * uniform_point - 1.0
    uniform_zero = to_unit(mix_bits(key_zero[None, None, :] ^ pert_seeds[:, :, None]))
    uniform_one = to_unit(mix_bits(key_one[None, None, :] ^ pert_seeds[:, :, None]))
    noise_draw = jnp.sqrt(-2.0 * jnp.log(uniform_zero)) * jnp.cos(2.0 * jnp.pi * uniform_one)
    shifted = (coords[:, None, :] + NOISE_SCALE * noise_draw).astype(jnp.bfloat16)
    shifted = shifted.reshape(count_points * count_samples, coords.shape[1])
    squares = lax.optimization_barrier(jnp.sum(noise_draw * noise_draw, axis=2)).reshape(count_points * count_samples)
    source = lax.optimization_barrier(jnp.sum(coef_part[None, :] * jnp.sin(jnp.pi * coords), axis=1)) / math.sqrt(D)
    return (shifted, squares, source)

def hidden_pass(pre_first, squares, source, w2, w3, count_samples):
    hidden_one = jnp.tanh(pre_first).astype(jnp.bfloat16)
    pre_second = lax.dot_general(hidden_one, w2, (((1,), (1,)), ((), ())), preferred_element_type=jnp.float32)
    hidden_two = jnp.tanh(pre_second).astype(jnp.bfloat16)
    values_out = READOUT * jnp.dot(hidden_two, w3, preferred_element_type=jnp.float32)
    stein_weight = (squares - D) / (NOISE_SCALE * NOISE_SCALE * count_samples)
    per_point = (stein_weight * values_out).reshape(-1, count_samples)
    residual = lax.optimization_barrier(jnp.sum(per_point, axis=1)) - source
    grad_values = (residual[:, None] * stein_weight.reshape(-1, count_samples)).reshape(-1)
    two_float = hidden_two.astype(jnp.float32)
    grad_readout = READOUT * lax.optimization_barrier(jnp.sum(grad_values[:, None] * two_float, axis=0))
    grad_pre_two = (READOUT * grad_values[:, None] * w3.astype(jnp.float32)[None, :] * (1.0 - two_float * two_float)).astype(jnp.bfloat16)
    grad_second = lax.dot_general(grad_pre_two, hidden_one, (((0,), (0,)), ((), ())), preferred_element_type=jnp.float32)
    grad_hidden = jnp.dot(grad_pre_two, w2, preferred_element_type=jnp.float32)
    one_float = hidden_one.astype(jnp.float32)
    grad_pre_one = (grad_hidden * (1.0 - one_float * one_float)).astype(jnp.bfloat16)
    grad_bias = lax.optimization_barrier(jnp.sum(grad_pre_one.astype(jnp.float32), axis=0))
    return (residual, grad_pre_one, grad_second, grad_bias, grad_readout)

def reference(point_seed, pert_seed, source_coef, w1, b1, w2, w3):
    column_hash = column_keys(jnp.arange(D, dtype=jnp.int32))
    block_count = POINTS // 8
    point_blocks = point_seed.reshape(block_count, 8)
    pert_blocks = pert_seed.reshape(block_count, 8, K)

    def forward_block(block_args):
        shifted, squares, source = perturbed_rows(block_args[0], block_args[1], column_hash, source_coef)
        pre_block = lax.dot_general(shifted, w1, (((1,), (1,)), ((), ())), preferred_element_type=jnp.float32)
        return (pre_block, squares, source)
    pre_blocks, square_blocks, source_blocks = lax.map(forward_block, (point_blocks, pert_blocks))
    pre_first = pre_blocks.reshape(POINTS * K, H) + b1[None, :]
    residual, grad_pre_one, grad_second, grad_bias, grad_readout = hidden_pass(pre_first, square_blocks.reshape(POINTS * K), source_blocks.reshape(POINTS), w2, w3, K)
    inner_count = PTS_DEV // 8
    grad_groups = grad_pre_one.reshape(N_PTS, inner_count, 8 * K, H)
    point_groups = point_seed.reshape(N_PTS, inner_count, 8)
    pert_groups = pert_seed.reshape(N_PTS, inner_count, 8, K)

    def block_term(accum, inner_args):
        shifted = perturbed_rows(inner_args[1], inner_args[2], column_hash, source_coef)[0]
        contrib = lax.dot_general(inner_args[0], shifted, (((0,), (0,)), ((), ())), preferred_element_type=jnp.float32)
        return (accum + contrib, None)

    def group_term(running, group_args):
        group_sum, _ = lax.scan(block_term, jnp.zeros((H, D), jnp.float32), group_args)
        rounded = lax.optimization_barrier(group_sum.astype(jnp.bfloat16)).astype(jnp.float32)
        return (running + rounded, None)
    summed, _ = lax.scan(group_term, jnp.zeros((H, D), jnp.float32), (grad_groups, point_groups, pert_groups))
    return (residual, summed.astype(jnp.bfloat16), grad_second, grad_bias, grad_readout)
```

```python
import functools
import math

import jax
import jax.numpy as jnp
import numpy as np
from jax import lax
from jax.experimental import pallas as pl
from jax.experimental.pallas import tpu as pltpu
from jax.sharding import PartitionSpec as P

D = 100000

HASH_FACTOR = 73244475
NOISE_SCALE = 2.0
READOUT = 0.0625
LANES = 128
GROUP = 256
MASK = 8388607
VMEM_BYTES = 56 * 1024 * 1024

C0, C1, C2, C3 = 6.283164044286755, -2.583571398038591, 0.3177373780982648, -0.017332380925367475
B0, B1, B2 = C0 / C3, C1 / C3, C2 / C3
SINE_SCALE = -C3 * 2.0**-23
LOG_SCALE = -2.0 * math.log(2.0) * (NOISE_SCALE * SINE_SCALE) ** 2


def shuffle_bits(bits):
    return bits ^ lax.shift_right_logical(bits, jnp.full_like(bits, 16))


def mix_tail(bits):
    bits = shuffle_bits(bits * HASH_FACTOR)
    return shuffle_bits(bits * HASH_FACTOR)


def mix_bits(bits):
    return mix_tail(shuffle_bits(bits))


def turn_wave(index):
    y = jnp.abs(index.astype(jnp.float32) + (0.5 - 4194304.0)) - 2097152.0
    s = (y * y) * 2.0**-42
    m = ((s + B2) * s + B1) * s + B0
    return y, -m


def tile_lanes(a, width):
    return jnp.concatenate([a] * (width // a.shape[1]), axis=1)


def column_keys(base, step, width):
    columns = lax.broadcasted_iota(jnp.int32, (8, width), 1) + step * width
    four = (columns + base) * 4
    return columns, [shuffle_bits(mix_bits(four + t)) for t in range(3)]


def draw(seeds, key_zero, key_one):
    width = key_zero.shape[1]
    seeds = tile_lanes(seeds, width)
    first = mix_tail(seeds ^ jnp.concatenate([key_zero] * 2, axis=0))
    second = mix_tail(seeds ^ jnp.concatenate([key_one] * 2, axis=0))
    u0 = ((first & MASK).astype(jnp.float32) + 0.5) * 2.0**-23
    n = jnp.log2(u0) * LOG_SCALE
    y, m = turn_wave(second & MASK)
    return ((n * lax.rsqrt(n)) * y) * m


def pieces(width):
    tiles = width // LANES
    parts = -(-tiles // 4)
    edges = [tiles * i // parts for i in range(parts + 1)]
    return [(a * LANES, b * LANES) for a, b in zip(edges, edges[1:])]


def point_rows(seeds, key, width):
    return mix_tail(tile_lanes(seeds, width) ^ key) & MASK


def coordinate(index):
    return (index.astype(jnp.float32) + (0.5 - 4194304.0)) * 2.0**-22


def forward_kernel(
    valid, base_ref, pert_ref, point_ref, coef_ref, w_prev, w_now,
    z_ref, pre_ref, sq_ref, src_ref, held_a, held_b, acc, keys, xs,
):
    step, last = pl.program_id(0), pl.num_programs(0) - 1
    rows, width = z_ref.shape
    points = point_ref.shape[0]
    samples = rows // points
    groups = rows // GROUP
    steps = -(-valid // width)
    pad = steps * width - valid

    @pl.when(step == 0)
    def _():
        acc[...] = jnp.zeros_like(acc)
        held_b[...] = jnp.zeros_like(held_b)
        sq_ref[...] = jnp.zeros_like(sq_ref)
        src_ref[...] = jnp.zeros_like(src_ref)

    columns, (key_zero, key_one, key_two) = column_keys(base_ref[0], step, width)
    keys[0:8] = key_zero
    keys[8:16] = key_one
    inside = columns < valid
    coef = jnp.where(inside, jnp.broadcast_to(coef_ref[...], (8, width)), 0.0)
    for at in range(0, points, 8):
        index = point_rows(point_ref[at:at + 8], key_two, width)
        xs[at:at + 8] = coordinate(index)
        y, m = turn_wave((index + 2097152) & MASK)
        term = ((y * SINE_SCALE) * m) * coef
        src_ref[at:at + 8] += sum(
            term[:, a:a + LANES] for a in range(0, width, LANES)
        )

    def weights(ref, of):
        cut = width - -(-pad // 16) * 16
        if cut == width:
            return ref[...]
        place = lax.broadcasted_iota(jnp.int32, (width - cut, ref.shape[1]), 0) + (of * width + cut)
        tail = jnp.where(place < valid, ref[cut:, :], jnp.zeros((), ref.dtype))
        return jnp.concatenate([ref[:cut, :], tail], axis=0)

    def multiply(group, held, ref, of):
        at = group * GROUP
        acc[at:at + GROUP, :] += jnp.dot(
            held[...], weights(ref, of), preferred_element_type=jnp.float32
        )

    for group in range(groups):
        held = (held_a, held_b)[group % 2]
        for at in range(0, GROUP, samples):
            row = group * GROUP + at
            point = row // samples
            seeds = pert_ref[row:row + samples]
            total = None
            for a, b in pieces(width):
                noise = draw(seeds, keys[0:8, a:b], keys[8:16, a:b])
                x = jnp.broadcast_to(xs[point:point + 1, a:b], (samples, b - a))
                z = (x + noise).astype(jnp.bfloat16)
                held[at:at + samples, a:b] = z
                z_ref[row:row + samples, a:b] = z
                square = noise * noise
                for c in range(a, b, LANES):
                    part = square[:, c - a:c - a + LANES]
                    if (steps - 1) * width + c + LANES > valid:
                        part = jnp.where(jnp.concatenate([inside[:, c:c + LANES]] * 2, axis=0), part, 0.0)
                    total = part if total is None else total + part
            sq_ref[row:row + samples] += total
        if group == 0:
            multiply(groups - 1, held_b, w_prev, jnp.maximum(step - 1, 0))
        else:
            multiply(group - 1, (held_b, held_a)[group % 2], w_now, step)

    @pl.when(step == last)
    def _():
        multiply(groups - 1, held_b, w_now, step)
        pre_ref[...] = acc[...].astype(pre_ref.dtype)


def redraw_kernel(first, base_ref, pert_ref, point_ref, z_ref, keys, xs):
    step = pl.program_id(0) + first
    rows, width = z_ref.shape
    points = point_ref.shape[0]
    samples = rows // points
    _, (key_zero, key_one, key_two) = column_keys(base_ref[0], step, width)
    keys[0:8] = key_zero
    keys[8:16] = key_one
    for at in range(0, points, 8):
        xs[at:at + 8] = coordinate(point_rows(point_ref[at:at + 8], key_two, width))

    @pl.loop(0, points // 8)
    def _(block):
        eight = xs[pl.ds(pl.multiple_of(block * 8, 8), 8)]
        for inner in range(8):
            row = pl.multiple_of((block * 8 + inner) * samples, samples)
            seeds = pert_ref[pl.ds(row, samples)]
            for a, b in pieces(width):
                noise = draw(seeds, keys[0:8, a:b], keys[8:16, a:b])
                x = jnp.broadcast_to(eight[inner:inner + 1, a:b], (samples, b - a))
                z_ref[pl.ds(row, samples), a:b] = (x + noise).astype(jnp.bfloat16)


def gradient_kernel(count, d_ref, *refs):
    z_refs, (keep_ref, send_ref) = refs[:count], refs[count:]
    blocks, _, hidden, _ = d_ref.shape
    half = hidden // 2
    left = jnp.concatenate(
        [d_ref[block, source] for source in range(count) for block in range(blocks)], axis=1
    )
    width = keep_ref.shape[0]
    stride = 256 if width % 256 == 0 else LANES
    for a in range(0, width, stride):
        z = jnp.concatenate([ref[:, a:a + stride] for ref in z_refs], axis=0)
        part = jnp.dot(left, z, preferred_element_type=jnp.float32).astype(jnp.bfloat16).T
        keep_ref[a:a + stride, :] = part[:, :half]
        send_ref[a:a + stride, :] = part[:, half:]


def join_kernel(*refs):
    keep_ref, got_ref, out_ref = refs[0], refs[1], refs[-1]
    out_ref[...] = (keep_ref[...].astype(jnp.float32) + got_ref[...].astype(jnp.float32)).astype(jnp.bfloat16)


def params():
    return pltpu.CompilerParams(dimension_semantics=("arbitrary",), vmem_limit_bytes=VMEM_BYTES)


def whole(shape):
    return pl.BlockSpec(shape, lambda s: (0,) * len(shape))


def lanes_of(seeds):
    return jnp.broadcast_to(shuffle_bits(seeds.reshape(-1))[:, None], (seeds.size, LANES))


def forward(base, pert, point, coef, w, width):
    valid, hidden = w.shape
    rows, points = pert.shape[0], point.shape[0]
    steps = -(-valid // width)
    smem = pl.BlockSpec(memory_space=pltpu.SMEM)
    return pl.pallas_call(
        functools.partial(forward_kernel, valid),
        grid=(steps,),
        in_specs=[
            smem, whole(pert.shape), whole(point.shape),
            pl.BlockSpec((1, width), lambda s: (0, s)),
            pl.BlockSpec((width, hidden), lambda s: (jnp.maximum(s - 1, 0), 0)),
            pl.BlockSpec((width, hidden), lambda s: (s, 0)),
        ],
        out_specs=[
            pl.BlockSpec((rows, width), lambda s: (0, s)),
            whole((rows, hidden)), whole((rows, LANES)), whole((points, LANES)),
        ],
        out_shape=[
            jax.ShapeDtypeStruct((rows, steps * width), jnp.bfloat16),
            jax.ShapeDtypeStruct((rows, hidden), jnp.bfloat16),
            jax.ShapeDtypeStruct((rows, LANES), jnp.float32),
            jax.ShapeDtypeStruct((points, LANES), jnp.float32),
        ],
        scratch_shapes=[
            pltpu.VMEM((GROUP, width), jnp.bfloat16),
            pltpu.VMEM((GROUP, width), jnp.bfloat16),
            pltpu.VMEM((rows, hidden), jnp.float32),
            pltpu.VMEM((16, width), jnp.int32),
            pltpu.VMEM((points, width), jnp.float32),
        ],
        compiler_params=params(),
        cost_estimate=pl.CostEstimate(
            flops=100 * rows * valid * 40, bytes_accessed=4 * rows * valid, transcendentals=2 * rows * valid
        ),
        name="forward",
    )(base, pert, point, coef, w, w)


def redraw(base, pert, point, width, first, count):
    rows, points = pert.shape[0], point.shape[0]
    return pl.pallas_call(
        functools.partial(redraw_kernel, first),
        grid=(count,),
        in_specs=[pl.BlockSpec(memory_space=pltpu.SMEM), whole(pert.shape), whole(point.shape)],
        out_specs=pl.BlockSpec((rows, width), lambda s: (0, s)),
        out_shape=jax.ShapeDtypeStruct((rows, count * width), jnp.bfloat16),
        scratch_shapes=[pltpu.VMEM((16, width), jnp.int32), pltpu.VMEM((points, width), jnp.float32)],
        compiler_params=params(),
        cost_estimate=pl.CostEstimate(
            flops=100 * rows * width * count * 40, bytes_accessed=2 * rows * width * count,
            transcendentals=2 * rows * width * count,
        ),
        name="redraw",
    )(base, pert, point)


def gradient(cotangent, own, others, width, first, count, valid):
    if count % 2 == 0 and first % 2 == 0:
        width, first, count = 2 * width, first // 2, count // 2
    rows = own.shape[0]
    half = cotangent.shape[2] // 2
    height = min(valid, (first + count) * width) - first * width
    return pl.pallas_call(
        functools.partial(gradient_kernel, 1 + len(others)),
        grid=(count,),
        in_specs=[whole(cotangent.shape), pl.BlockSpec((rows, width), lambda s: (0, s + first))]
        + [pl.BlockSpec((rows, width), lambda s: (0, s)) for _ in others],
        out_specs=[pl.BlockSpec((width, half), lambda s: (s, 0))] * 2,
        out_shape=[jax.ShapeDtypeStruct((height, half), jnp.bfloat16)] * 2,
        compiler_params=params(),
        cost_estimate=pl.CostEstimate(
            flops=4 * half * rows * (1 + len(others)) * width * count,
            bytes_accessed=2 * rows * (1 + len(others)) * width * count, transcendentals=0,
        ),
        name="gradient",
    )(cotangent, own, *others)


def join(keep, got, before, width, first, valid):
    height, half = keep.shape
    count = -(-height // width)
    specs = [pl.BlockSpec((width, half), lambda s: (s, 0))] * 2
    operands, aliases = [keep, got], {}
    if before is not None:
        specs, operands, aliases = specs + [pl.BlockSpec(memory_space=pl.ANY)], operands + [before], {2: 0}
    return pl.pallas_call(
        join_kernel,
        grid=(count,),
        in_specs=specs,
        out_specs=pl.BlockSpec((width, half), lambda s: (s + first, 0)),
        out_shape=jax.ShapeDtypeStruct((valid, half), jnp.bfloat16),
        input_output_aliases=aliases,
        compiler_params=params(),
        cost_estimate=pl.CostEstimate(flops=height * half, bytes_accessed=6 * height * half, transcendentals=0),
        name="join",
    )(*operands)


def hidden_pass(pre_first, squares, source, w2, w3, count_samples):
    hidden_one = jnp.tanh(pre_first).astype(jnp.bfloat16)
    pre_second = lax.dot_general(
        hidden_one, w2, (((1,), (1,)), ((), ())), preferred_element_type=jnp.float32
    )
    hidden_two = jnp.tanh(pre_second).astype(jnp.bfloat16)
    values_out = READOUT * jnp.dot(hidden_two, w3, preferred_element_type=jnp.float32)
    stein_weight = (squares - D) / (NOISE_SCALE * NOISE_SCALE * count_samples)
    per_point = (stein_weight * values_out).reshape(-1, count_samples)
    residual = jnp.sum(per_point, axis=1) - source
    grad_values = (residual[:, None] * stein_weight.reshape(-1, count_samples)).reshape(-1)
    two_float = hidden_two.astype(jnp.float32)
    grad_readout = READOUT * jnp.sum(grad_values[:, None] * two_float, axis=0)
    grad_pre_two = (
        READOUT
        * grad_values[:, None]
        * w3.astype(jnp.float32)[None, :]
        * (1.0 - two_float * two_float)
    ).astype(jnp.bfloat16)
    grad_hidden = jnp.dot(grad_pre_two, w2, preferred_element_type=jnp.float32)
    one_float = hidden_one.astype(jnp.float32)
    grad_pre_one = (grad_hidden * (1.0 - one_float * one_float)).astype(jnp.bfloat16)
    return (residual, grad_pre_one, grad_readout, hidden_one, grad_pre_two)


def block_width(valid):
    tiles = -(-valid // LANES)
    best = min((8, 7, 6, 5), key=lambda t: -(-tiles // t) * t)
    return best * LANES


def tie(first, second):
    return lax.optimization_barrier((first, second))


def shards(point_seed, pert_seed, source_coef, w1, b1, w2, w3):
    coord_count = lax.axis_size("coord")
    pts_count = lax.axis_size("pts")
    chips = pts_count // 2
    hidden, valid = w1.shape
    points_here, samples = pert_seed.shape
    rows_here = points_here * samples
    rows_local = rows_here // coord_count
    points_local = points_here // coord_count
    coord_index = lax.axis_index("coord")
    pts_index = lax.axis_index("pts")
    share = hidden // pts_count
    width = block_width(valid)
    steps = -(-valid // width)
    base = (coord_index * valid).astype(jnp.int32).reshape(1)

    def shift(a, by):
        return jax.tree.map(
            lambda leaf: lax.ppermute(
                leaf, "pts", [(i, (i + 2 * by) % pts_count) for i in range(pts_count)]
            ), a,
        )

    other_seeds = [shift((pert_seed, point_seed), by) for by in range(1, chips)]

    pert, point = lanes_of(pert_seed), lanes_of(point_seed)
    own, pre, squares, source = forward(base, pert, point, source_coef[None, :], w1.T, width)
    other_seeds, pre = tie(other_seeds, pre)
    others_in = [(lanes_of(a), lanes_of(b)) for a, b in other_seeds]

    pre_local = lax.psum_scatter(pre, "coord", scatter_dimension=0, tiled=True)
    sums = jnp.concatenate(
        [jnp.sum(squares, axis=1) / NOISE_SCALE**2, jnp.sum(source, axis=1) / math.sqrt(D)]
    )
    sums = jnp.sum(lax.all_gather(sums, "coord", axis=0), axis=0)
    squares_local = lax.dynamic_slice_in_dim(sums, coord_index * rows_local, rows_local, 0)
    source_local = lax.dynamic_slice_in_dim(sums, rows_here + coord_index * points_local, points_local, 0)

    early = steps // 2 + (steps // 2) % 2
    cuts = [(0, early), (early, steps - early)]
    drawn = [[redraw(base, a, b, width, *cuts[0]) for a, b in others_in]]

    residual, grad_pre_one, grad_readout, hidden_one, grad_pre_two = hidden_pass(
        pre_local.astype(jnp.float32) + b1[None, :], squares_local, source_local, w2, w3, samples
    )
    turned = grad_pre_one.T

    def share_of(index):
        return [lax.dynamic_slice_in_dim(turned, i * share, share, 0) for i in (index, index ^ 1)]

    sent = [jnp.concatenate(share_of((pts_index + 2 * by) % pts_count), axis=0) for by in range(chips)]
    mine = jnp.stack([sent[0]] + [shift(sent[by], by) for by in range(1, chips)])
    others_in, mine = tie(others_in, mine)
    cotangent = lax.all_gather(mine, "coord", axis=0)
    blocks = rows_here // LANES
    if rows_local != LANES:
        cotangent = cotangent.transpose(1, 2, 0, 3).reshape(chips, 2 * share, blocks, LANES)
        cotangent = cotangent.transpose(2, 0, 1, 3)
    drawn.append([redraw(base, a, b, width, *cuts[1]) for a, b in others_in])

    (hidden_one, grad_pre_two), cotangent = tie((hidden_one, grad_pre_two), cotangent)
    grad_second = lax.dot_general(
        grad_pre_two, hidden_one, (((0,), (0,)), ((), ())), preferred_element_type=jnp.float32
    )
    grad_bias = jnp.sum(grad_pre_one.astype(jnp.float32), axis=0)
    small = jnp.concatenate(
        [grad_second, grad_bias[:, None], grad_readout[:, None], jnp.zeros((hidden, LANES - 2), jnp.float32)], axis=1
    ).astype(jnp.bfloat16)
    small = lax.psum_scatter(small, "coord", scatter_dimension=0, tiled=True)
    small = lax.psum(small, "pts").astype(jnp.float32)

    out = None
    swap = [(i, i ^ 1) for i in range(pts_count)]
    for (first, count), z in zip(cuts, drawn):
        keep, send = gradient(cotangent, own, z, width, first, count, valid)
        got = lax.ppermute(send, "pts", swap)
        wide = 2 * width if count % 2 == 0 and first % 2 == 0 else width
        out = join(keep, got, out, wide, first * width // wide, valid)
    return (residual, out.T, small[:, :hidden], small[:, hidden], small[:, hidden + 1])


def solution(mesh):
    return jax.shard_map(
        shards,
        mesh=mesh,
        in_specs=(P("pts"), P("pts", None), P("coord"), P(None, "coord"), P(), P(), P()),
        out_specs=(
            P(("pts", "coord")),
            P("pts", "coord"),
            P("coord", None),
            P("coord"),
            P("coord"),
        ),
        check_vma=False,
    )
```

```python
import functools
import math

import jax
import jax.numpy as jnp
import numpy as np
from jax import lax
from jax.experimental import pallas as pl
from jax.experimental.pallas import tpu as pltpu
from jax.sharding import PartitionSpec as P

D = 100000

HASH_FACTOR = 73244475
NOISE_SCALE = 2.0
READOUT = 0.0625
LANES = 128
GROUP = 256
MASK = 8388607
VMEM_BYTES = 56 * 1024 * 1024

C0, C1, C2, C3 = 6.283164044286755, -2.583571398038591, 0.3177373780982648, -0.017332380925367475
B0, B1, B2 = C0 / C3, C1 / C3, C2 / C3
SINE_SCALE = -C3 * 2.0**-23
LOG_SCALE = -2.0 * math.log(2.0) * (NOISE_SCALE * SINE_SCALE) ** 2


def shuffle_bits(bits):
    return bits ^ lax.shift_right_logical(bits, jnp.full_like(bits, 16))


def mix_tail(bits):
    bits = shuffle_bits(bits * HASH_FACTOR)
    return shuffle_bits(bits * HASH_FACTOR)


def mix_bits(bits):
    return mix_tail(shuffle_bits(bits))


def turn_wave(index):
    y = jnp.abs(index.astype(jnp.float32) + (0.5 - 4194304.0)) - 2097152.0
    s = (y * y) * 2.0**-42
    m = ((s + B2) * s + B1) * s + B0
    return y, -m


def tile_lanes(a, width):
    return jnp.concatenate([a] * (width // a.shape[1]), axis=1)


def column_keys(base, step, width):
    columns = lax.broadcasted_iota(jnp.int32, (8, width), 1) + step * width
    four = (columns + base) * 4
    return columns, [shuffle_bits(mix_bits(four + t)) for t in range(3)]


def draw(seeds, key_zero, key_one):
    width = key_zero.shape[1]
    seeds = tile_lanes(seeds, width)
    first = mix_tail(seeds ^ jnp.concatenate([key_zero] * 2, axis=0))
    second = mix_tail(seeds ^ jnp.concatenate([key_one] * 2, axis=0))
    u0 = ((first & MASK).astype(jnp.float32) + 0.5) * 2.0**-23
    n = jnp.log2(u0) * LOG_SCALE
    y, m = turn_wave(second & MASK)
    return ((n * lax.rsqrt(n)) * y) * m


def pieces(width):
    tiles = width // LANES
    parts = -(-tiles // 2)
    edges = [tiles * i // parts for i in range(parts + 1)]
    return [(a * LANES, b * LANES) for a, b in zip(edges, edges[1:])]


def point_rows(seeds, key, width):
    return mix_tail(tile_lanes(seeds, width) ^ key) & MASK


def coordinate(index):
    return (index.astype(jnp.float32) + (0.5 - 4194304.0)) * 2.0**-22


def forward_kernel(
    valid, base_ref, pert_ref, point_ref, coef_ref, w_prev, w_now,
    z_ref, pre_ref, sums_ref, held_a, held_b, acc, keys, xs, sq_ref, src_ref,
):
    step, last = pl.program_id(0), pl.num_programs(0) - 1
    rows, width = z_ref.shape
    points = point_ref.shape[0]
    samples = rows // points
    groups = rows // GROUP
    steps = -(-valid // width)
    pad = steps * width - valid

    @pl.when(step == 0)
    def _():
        acc[...] = jnp.zeros_like(acc)
        held_b[...] = jnp.zeros_like(held_b)
        sq_ref[...] = jnp.zeros_like(sq_ref)
        src_ref[...] = jnp.zeros_like(src_ref)

    columns, (key_zero, key_one, key_two) = column_keys(base_ref[0], step, width)
    keys[0:8] = key_zero
    keys[8:16] = key_one
    inside = columns < valid
    coef = jnp.where(inside, jnp.broadcast_to(coef_ref[...], (8, width)), 0.0)
    for at in range(0, points, 8):
        index = point_rows(point_ref[at:at + 8], key_two, width)
        xs[at:at + 8] = coordinate(index)
        y, m = turn_wave((index + 2097152) & MASK)
        term = ((y * SINE_SCALE) * m) * coef
        src_ref[at:at + 8] += sum(
            term[:, a:a + LANES] for a in range(0, width, LANES)
        )

    cut = width - -(-pad // 16) * 16

    def multiply(group, part, held, ref, of):
        at, left = group * GROUP, part * GROUP
        w = ref[:, left:left + GROUP]
        if pad:
            place = lax.broadcasted_iota(jnp.int32, (width - cut, GROUP), 0) + (of * width + cut)
            tail = jnp.where(place < valid, w[cut:], jnp.zeros((), w.dtype))
            w = jnp.concatenate([w[:cut], tail], axis=0)
        acc[at:at + GROUP, left:left + GROUP] += jnp.dot(
            held[...], w, preferred_element_type=jnp.float32
        )

    parts = acc.shape[1] // GROUP
    group_points = GROUP // samples

    for group in range(groups):
        held = (held_a, held_b)[group % 2]
        other = (held_b, held_a)[group % 2]
        for number in range(group_points):
            if number % (group_points // parts) == 0:
                part = number // (group_points // parts)
                if group == 0:
                    multiply(groups - 1, part, other, w_prev, jnp.maximum(step - 1, 0))
                else:
                    multiply(group - 1, part, other, w_now, step)
            at = number * samples
            row = group * GROUP + at
            point = row // samples
            seeds = pert_ref[row:row + samples]
            total = None
            for a, b in pieces(width):
                noise = draw(seeds, keys[0:8, a:b], keys[8:16, a:b])
                x = jnp.broadcast_to(xs[point:point + 1, a:b], (samples, b - a))
                z = (x + noise).astype(jnp.bfloat16)
                held[at:at + samples, a:b] = z
                z_ref[row:row + samples, a:b] = z
                square = noise * noise
                for c in range(a, b, LANES):
                    cell = square[:, c - a:c - a + LANES]
                    if (steps - 1) * width + c + LANES > valid:
                        cell = jnp.where(jnp.concatenate([inside[:, c:c + LANES]] * 2, axis=0), cell, 0.0)
                    total = cell if total is None else total + cell
            sq_ref[row:row + samples] += total

    @pl.when(step == last)
    def _():
        for part in range(parts):
            multiply(groups - 1, part, held_b, w_now, step)
        pre_ref[...] = acc[...].astype(pre_ref.dtype)
        sums_ref[...] = jnp.zeros_like(sums_ref)
        for block in range(rows // LANES):
            square = jnp.sum(sq_ref[block * LANES:(block + 1) * LANES].T, axis=0, keepdims=True)
            sums_ref[block:block + 1] = square / NOISE_SCALE**2
        sums_ref[8:9, :points] = jnp.sum(src_ref[...].T, axis=0, keepdims=True) / math.sqrt(D)


def redraw_kernel(first, base_ref, pert_ref, point_ref, _, z_ref, mark_ref, keys, xs):
    step = pl.program_id(0) + first
    rows, width = z_ref.shape
    points = point_ref.shape[0]
    samples = rows // points
    _, (key_zero, key_one, key_two) = column_keys(base_ref[0], step, width)
    keys[0:8] = key_zero
    keys[8:16] = key_one
    mark_ref[...] = jnp.zeros_like(mark_ref)
    for at in range(0, points, 8):
        xs[at:at + 8] = coordinate(point_rows(point_ref[at:at + 8], key_two, width))

    @pl.loop(0, points // 8)
    def _(block):
        eight = xs[pl.ds(pl.multiple_of(block * 8, 8), 8)]
        for inner in range(8):
            row = pl.multiple_of((block * 8 + inner) * samples, samples)
            seeds = pert_ref[pl.ds(row, samples)]
            for a, b in pieces(width):
                noise = draw(seeds, keys[0:8, a:b], keys[8:16, a:b])
                x = jnp.broadcast_to(eight[inner:inner + 1, a:b], (samples, b - a))
                z_ref[pl.ds(row, samples), a:b] = (x + noise).astype(jnp.bfloat16)


def gradient_kernel(count, per, _, d_ref, *refs):
    z_refs, (keep_ref, send_ref, left) = refs[:count], refs[count:]
    blocks, _, hidden = d_ref.shape
    half = hidden // 2
    together = LANES // per

    @pl.when(pl.program_id(0) == 0)
    def _():
        for source in range(count):
            for block in range(0, blocks, together):
                at = source * blocks * per + block * per
                rows = jnp.concatenate(
                    [d_ref[block + i, source * per:(source + 1) * per] for i in range(together)], axis=0
                )
                left[:, at:at + LANES] = rows.T

    width = keep_ref.shape[0]
    stride = 256 if width % 256 == 0 else LANES
    for a in range(0, width, stride):
        z = jnp.concatenate([ref[:, a:a + stride] for ref in z_refs], axis=0)
        part = jnp.dot(left[...], z, preferred_element_type=jnp.float32).astype(jnp.bfloat16).T
        keep_ref[a:a + stride, :] = part[:, :half]
        send_ref[a:a + stride, :] = part[:, half:]


def join_kernel(*refs):
    keep_ref, got_ref, out_ref = refs[0], refs[1], refs[-1]
    out_ref[...] = (keep_ref[...].astype(jnp.float32) + got_ref[...].astype(jnp.float32)).astype(jnp.bfloat16)


def params():
    return pltpu.CompilerParams(dimension_semantics=("arbitrary",), vmem_limit_bytes=VMEM_BYTES)


def whole(shape):
    return pl.BlockSpec(shape, lambda s: (0,) * len(shape))


def lanes_of(seeds):
    return jnp.broadcast_to(shuffle_bits(seeds.reshape(-1))[:, None], (seeds.size, LANES))


def forward(base, pert, point, coef, w, width):
    valid, hidden = w.shape
    rows, points = pert.shape[0], point.shape[0]
    steps = -(-valid // width)
    smem = pl.BlockSpec(memory_space=pltpu.SMEM)
    return pl.pallas_call(
        functools.partial(forward_kernel, valid),
        grid=(steps,),
        in_specs=[
            smem, whole(pert.shape), whole(point.shape),
            pl.BlockSpec((1, width), lambda s: (0, s)),
            pl.BlockSpec((width, hidden), lambda s: (jnp.maximum(s - 1, 0), 0)),
            pl.BlockSpec((width, hidden), lambda s: (s, 0)),
        ],
        out_specs=[
            pl.BlockSpec((rows, width), lambda s: (0, s)),
            whole((rows, hidden)), whole((16, LANES)),
        ],
        out_shape=[
            jax.ShapeDtypeStruct((rows, steps * width), jnp.bfloat16),
            jax.ShapeDtypeStruct((rows, hidden), jnp.bfloat16),
            jax.ShapeDtypeStruct((16, LANES), jnp.float32),
        ],
        scratch_shapes=[
            pltpu.VMEM((GROUP, width), jnp.bfloat16),
            pltpu.VMEM((GROUP, width), jnp.bfloat16),
            pltpu.VMEM((rows, hidden), jnp.float32),
            pltpu.VMEM((16, width), jnp.int32),
            pltpu.VMEM((points, width), jnp.float32),
            pltpu.VMEM((rows, LANES), jnp.float32),
            pltpu.VMEM((points, LANES), jnp.float32),
        ],
        compiler_params=params(),
        cost_estimate=pl.CostEstimate(
            flops=100 * rows * valid * 40, bytes_accessed=4 * rows * valid, transcendentals=2 * rows * valid
        ),
        name="forward",
    )(base, pert, point, coef, w, w)


def redraw(base, pert, point, after, width, first, count):
    rows, points = pert.shape[0], point.shape[0]
    return pl.pallas_call(
        functools.partial(redraw_kernel, first),
        grid=(count,),
        in_specs=[
            pl.BlockSpec(memory_space=pltpu.SMEM), whole(pert.shape), whole(point.shape),
            pl.BlockSpec(memory_space=pl.ANY),
        ],
        out_specs=[pl.BlockSpec((rows, width), lambda s: (0, s)), whole((8, LANES))],
        out_shape=[
            jax.ShapeDtypeStruct((rows, count * width), jnp.bfloat16),
            jax.ShapeDtypeStruct((8, LANES), jnp.float32),
        ],
        scratch_shapes=[pltpu.VMEM((16, width), jnp.int32), pltpu.VMEM((points, width), jnp.float32)],
        compiler_params=params(),
        cost_estimate=pl.CostEstimate(
            flops=100 * rows * width * count * 40, bytes_accessed=2 * rows * width * count,
            transcendentals=2 * rows * width * count,
        ),
        name="redraw",
    )(base, pert, point, after)


def gradient(after, cotangent, per, own, others, width, first, count, valid):
    if count % 2 == 0 and first % 2 == 0:
        width, first, count = 2 * width, first // 2, count // 2
    rows = own.shape[0]
    half = cotangent.shape[2] // 2
    height = min(valid, (first + count) * width) - first * width
    return pl.pallas_call(
        functools.partial(gradient_kernel, 1 + len(others), per),
        grid=(count,),
        in_specs=[pl.BlockSpec(memory_space=pl.ANY), whole(cotangent.shape), pl.BlockSpec((rows, width), lambda s: (0, s + first))]
        + [pl.BlockSpec((rows, width), lambda s: (0, s)) for _ in others],
        out_specs=[pl.BlockSpec((width, half), lambda s: (s, 0))] * 2,
        out_shape=[jax.ShapeDtypeStruct((height, half), jnp.bfloat16)] * 2,
        scratch_shapes=[pltpu.VMEM((2 * half, (1 + len(others)) * rows), jnp.bfloat16)],
        compiler_params=params(),
        cost_estimate=pl.CostEstimate(
            flops=4 * half * rows * (1 + len(others)) * width * count,
            bytes_accessed=2 * rows * (1 + len(others)) * width * count, transcendentals=0,
        ),
        name="gradient",
    )(after, cotangent, own, *others)


def join(keep, got, before, width, first, valid):
    height, half = keep.shape
    count = -(-height // width)
    specs = [pl.BlockSpec((width, half), lambda s: (s, 0))] * 2
    operands, aliases = [keep, got], {}
    if before is not None:
        specs, operands, aliases = specs + [pl.BlockSpec(memory_space=pl.ANY)], operands + [before], {2: 0}
    return pl.pallas_call(
        join_kernel,
        grid=(count,),
        in_specs=specs,
        out_specs=pl.BlockSpec((width, half), lambda s: (s + first, 0)),
        out_shape=jax.ShapeDtypeStruct((valid, half), jnp.bfloat16),
        input_output_aliases=aliases,
        compiler_params=params(),
        cost_estimate=pl.CostEstimate(flops=height * half, bytes_accessed=6 * height * half, transcendentals=0),
        name="join",
    )(*operands)


def hidden_pass(pre_first, squares, source, w2, w3, count_samples):
    hidden_one = jnp.tanh(pre_first).astype(jnp.bfloat16)
    pre_second = lax.dot_general(
        hidden_one, w2, (((1,), (1,)), ((), ())), preferred_element_type=jnp.float32
    )
    hidden_two = jnp.tanh(pre_second).astype(jnp.bfloat16)
    values_out = READOUT * jnp.dot(hidden_two, w3, preferred_element_type=jnp.float32)
    stein_weight = (squares - D) / (NOISE_SCALE * NOISE_SCALE * count_samples)
    per_point = (stein_weight * values_out).reshape(-1, count_samples)
    residual = jnp.sum(per_point, axis=1) - source
    grad_values = (residual[:, None] * stein_weight.reshape(-1, count_samples)).reshape(-1)
    two_float = hidden_two.astype(jnp.float32)
    grad_readout = READOUT * jnp.sum(grad_values[:, None] * two_float, axis=0)
    grad_pre_two = (
        READOUT
        * grad_values[:, None]
        * w3.astype(jnp.float32)[None, :]
        * (1.0 - two_float * two_float)
    ).astype(jnp.bfloat16)
    grad_hidden = jnp.dot(grad_pre_two, w2, preferred_element_type=jnp.float32)
    one_float = hidden_one.astype(jnp.float32)
    grad_pre_one = (grad_hidden * (1.0 - one_float * one_float)).astype(jnp.bfloat16)
    return (residual, grad_pre_one, grad_readout, hidden_one, grad_pre_two)


def block_width(valid):
    tiles = -(-valid // LANES)
    best = min((8, 7, 6, 5), key=lambda t: -(-tiles // t) * t)
    return best * LANES


def tie(first, second):
    return lax.optimization_barrier((first, second))


def shards(point_seed, pert_seed, source_coef, w1, b1, w2, w3):
    coord_count = lax.axis_size("coord")
    pts_count = lax.axis_size("pts")
    chips = pts_count // 2
    hidden, valid = w1.shape
    points_here, samples = pert_seed.shape
    rows_here = points_here * samples
    rows_local = rows_here // coord_count
    points_local = points_here // coord_count
    coord_index = lax.axis_index("coord")
    pts_index = lax.axis_index("pts")
    share = hidden // pts_count
    width = block_width(valid)
    steps = -(-valid // width)
    base = (coord_index * valid).astype(jnp.int32).reshape(1)

    def shift(a, by):
        return jax.tree.map(
            lambda leaf: lax.ppermute(
                leaf, "pts", [(i, (i + 2 * by) % pts_count) for i in range(pts_count)]
            ), a,
        )

    other_seeds = [shift((pert_seed, point_seed), by) for by in range(1, chips)]

    pert, point = lanes_of(pert_seed), lanes_of(point_seed)
    own, pre, sums = forward(base, pert, point, source_coef[None, :], w1.T, width)
    others_in = [(lanes_of(a), lanes_of(b)) for a, b in other_seeds]

    sums = lax.all_gather(sums, "coord", axis=0)
    pre_local = lax.psum_scatter(pre, "coord", scatter_dimension=0, tiled=True)

    early = steps // 2 + (steps // 2) % 2
    cuts = [(0, early), (early, steps - early)]
    drawn = [[redraw(base, a, b, pre, width, *cuts[0]) for a, b in others_in]]
    (pre_local, sums), _ = tie((pre_local, sums), [mark for _, mark in drawn[0]])

    sums = jnp.sum(sums, axis=0)
    squares_local = lax.dynamic_slice_in_dim(sums[:8].reshape(-1), coord_index * rows_local, rows_local, 0)
    source_local = lax.dynamic_slice_in_dim(sums[8], coord_index * points_local, points_local, 0)
    residual, grad_pre_one, grad_readout, hidden_one, grad_pre_two = hidden_pass(
        pre_local.astype(jnp.float32) + b1[None, :], squares_local, source_local, w2, w3, samples
    )

    def share_of(index):
        return jnp.concatenate(
            [lax.dynamic_slice_in_dim(grad_pre_one, i * share, share, 1) for i in (index, index ^ 1)], axis=1
        )

    sent = [share_of((pts_index + 2 * by) % pts_count) for by in range(chips)]
    readout_rows = grad_readout.astype(jnp.bfloat16).reshape(-1, 2 * share)
    readout_rows = jnp.pad(readout_rows, ((0, 16 - readout_rows.shape[0]), (0, 0)))
    mine = jnp.concatenate([sent[0]] + [shift(sent[by], by) for by in range(1, chips)] + [readout_rows], axis=0)
    cotangent = lax.all_gather(mine, "coord", axis=0)
    drawn.append([redraw(base, a, b, mine, width, *cuts[1]) for a, b in others_in])

    def rotate(a, by):
        return lax.ppermute(a, "pts", [(i, (i + by) % pts_count) for i in range(pts_count)])

    grad_second = lax.dot_general(
        grad_pre_two, hidden_one, (((0,), (0,)), ((), ())), preferred_element_type=jnp.float32
    ).astype(jnp.bfloat16)
    quarter = hidden // coord_count // pts_count
    grad_second = grad_second.reshape(coord_count, pts_count, quarter, hidden)

    def second_part(index):
        return lax.dynamic_slice_in_dim(grad_second, index, 1, 1).reshape(coord_count * quarter, hidden)

    second = second_part(pts_index).astype(jnp.float32)
    for by in range(1, pts_count):
        second += rotate(second_part((pts_index + by) % pts_count), by).astype(jnp.float32)
    second, _ = tie(second.astype(jnp.bfloat16), cotangent[0, :16])
    scattered = lax.psum_scatter(second, "coord", scatter_dimension=0, tiled=True)
    second = lax.all_gather(scattered, "pts", axis=0, tiled=True).astype(jnp.float32)

    wide = cotangent.astype(jnp.float32)
    bias_half = jnp.sum(wide[:, :chips * rows_local], axis=(0, 1))
    readout = jnp.sum(wide[:, chips * rows_local:chips * rows_local + pts_count // 2], axis=0).reshape(-1)
    bias = jnp.zeros((hidden,), jnp.float32)
    for number, index in enumerate((pts_index, pts_index ^ 1)):
        bias = lax.dynamic_update_slice_in_dim(bias, bias_half[number * share:(number + 1) * share], index * share, 0)
    vectors = jnp.stack([bias, readout]).reshape(-1, LANES)
    vectors = vectors + sum(rotate(vectors, by) for by in range(1, pts_count))
    bias, readout = (
        lax.dynamic_slice_in_dim(v, coord_index * (hidden // coord_count), hidden // coord_count, 0)
        for v in vectors.reshape(2, hidden)
    )

    out = None
    swap = [(i, i ^ 1) for i in range(pts_count)]
    for (first, count), z, after in zip(cuts, drawn, (mine, scattered)):
        keep, send = gradient(after, cotangent, rows_local, own, [a for a, _ in z], width, first, count, valid)
        got = lax.ppermute(send, "pts", swap)
        wide = 2 * width if count % 2 == 0 and first % 2 == 0 else width
        out = join(keep, got, out, wide, first * width // wide, valid)
    return (residual, out.T, second, bias, readout)


def solution(mesh):
    return jax.shard_map(
        shards,
        mesh=mesh,
        in_specs=(P("pts"), P("pts", None), P("coord"), P(None, "coord"), P(), P(), P()),
        out_specs=(
            P(("pts", "coord")),
            P("pts", "coord"),
            P("coord", None),
            P("coord"),
            P("coord"),
        ),
        check_vma=False,
    )
```

```python
import functools
import math

import jax
import jax.numpy as jnp
import numpy as np
from jax import lax
from jax.experimental import pallas as pl
from jax.experimental.pallas import tpu as pltpu
from jax.sharding import PartitionSpec as P

D = 100000

HASH_FACTOR = 73244475
NOISE_SCALE = 2.0
READOUT = 0.0625
LANES = 128
GROUP = 256
MASK = 8388607
VMEM_BYTES = 56 * 1024 * 1024

C0, C1, C2, C3 = 6.283164044286755, -2.583571398038591, 0.3177373780982648, -0.017332380925367475
B0, B1, B2 = C0 / C3, C1 / C3, C2 / C3
SINE_SCALE = -C3 * 2.0**-23
LOG_SCALE = -2.0 * math.log(2.0) * (NOISE_SCALE * SINE_SCALE) ** 2


def shuffle_bits(bits):
    return bits ^ lax.shift_right_logical(bits, jnp.full_like(bits, 16))


def mix_tail(bits):
    bits = shuffle_bits(bits * HASH_FACTOR)
    return shuffle_bits(bits * HASH_FACTOR)


def mix_bits(bits):
    return mix_tail(shuffle_bits(bits))


def turn_wave(index):
    y = 2097152.0 - jnp.abs(index.astype(jnp.float32) + (0.5 - 4194304.0))
    s = (y * y) * 2.0**-42
    m = ((s + B2) * s + B1) * s + B0
    return y, m


def tile_lanes(a, width):
    return jnp.concatenate([a] * (width // a.shape[1]), axis=1)


def column_keys(base, step, width):
    columns = lax.broadcasted_iota(jnp.int32, (8, width), 1) + step * width
    four = (columns + base) * 4
    return columns, [shuffle_bits(mix_bits(four + t)) for t in range(3)]


def draw(seeds, key_zero, key_one):
    width = key_zero.shape[1]
    seeds = tile_lanes(seeds, width)
    first = mix_tail(seeds ^ jnp.concatenate([key_zero] * 2, axis=0))
    second = mix_tail(seeds ^ jnp.concatenate([key_one] * 2, axis=0))
    u0 = ((first & MASK).astype(jnp.float32) + 0.5) * 2.0**-23
    n = jnp.log2(u0) * LOG_SCALE
    y, m = turn_wave(second & MASK)
    return ((n * lax.rsqrt(n)) * y) * m


def pieces(width):
    tiles = width // LANES
    parts = -(-tiles // 2)
    edges = [tiles * i // parts for i in range(parts + 1)]
    return [(a * LANES, b * LANES) for a, b in zip(edges, edges[1:])]


def point_rows(seeds, key, width):
    return mix_tail(tile_lanes(seeds, width) ^ key) & MASK


def coordinate(index):
    return (index.astype(jnp.float32) + (0.5 - 4194304.0)) * 2.0**-22


def forward_kernel(
    valid, base_ref, pert_ref, point_ref, coef_ref, w_prev, w_now, z_ref, *refs,
):
    near_ref, far_ref, held_a, held_b, acc, keys, xs, sq_ref, src_ref, sums = refs
    step, last = pl.program_id(0), pl.num_programs(0) - 1
    rows, width = z_ref.shape
    points = point_ref.shape[0]
    samples = rows // points
    groups = rows // GROUP
    steps = -(-valid // width)
    pad = steps * width - valid

    @pl.when(step == 0)
    def _():
        acc[...] = jnp.zeros_like(acc)
        held_b[...] = jnp.zeros_like(held_b)
        sq_ref[...] = jnp.zeros_like(sq_ref)
        src_ref[...] = jnp.zeros_like(src_ref)

    columns, (key_zero, key_one, key_two) = column_keys(base_ref[0], step, width)
    keys[0:8] = key_zero
    keys[8:16] = key_one
    inside = columns < valid
    coef = jnp.where(inside, jnp.broadcast_to(coef_ref[...], (8, width)), 0.0)
    for at in range(0, points, 8):
        index = point_rows(point_ref[at:at + 8], key_two, width)
        xs[at:at + 8] = coordinate(index)
        y, m = turn_wave((index + 2097152) & MASK)
        term = ((y * SINE_SCALE) * m) * coef
        src_ref[at:at + 8] += sum(
            term[:, a:a + LANES] for a in range(0, width, LANES)
        )

    cut = width - -(-pad // 16) * 16

    def multiply(group, part, held, ref, of):
        at, left = group * GROUP, part * GROUP
        w = ref[:, left:left + GROUP]
        if pad:
            place = lax.broadcasted_iota(jnp.int32, (width - cut, GROUP), 0) + (of * width + cut)
            tail = jnp.where(place < valid, w[cut:], jnp.zeros((), w.dtype))
            w = jnp.concatenate([w[:cut], tail], axis=0)
        acc[at:at + GROUP, left:left + GROUP] += jnp.dot(
            held[...], w, preferred_element_type=jnp.float32
        )

    parts = acc.shape[1] // GROUP
    group_points = GROUP // samples

    for group in range(groups):
        held = (held_a, held_b)[group % 2]
        other = (held_b, held_a)[group % 2]
        for number in range(group_points):
            if number % (group_points // parts) == 0:
                part = number // (group_points // parts)
                if group == 0:
                    multiply(groups - 1, part, other, w_prev, jnp.maximum(step - 1, 0))
                else:
                    multiply(group - 1, part, other, w_now, step)
            at = number * samples
            row = group * GROUP + at
            point = row // samples
            seeds = pert_ref[row:row + samples]
            total = None
            for a, b in pieces(width):
                noise = draw(seeds, keys[0:8, a:b], keys[8:16, a:b])
                x = jnp.broadcast_to(xs[point:point + 1, a:b], (samples, b - a))
                z = (x + noise).astype(jnp.bfloat16)
                held[at:at + samples, a:b] = z
                z_ref[row:row + samples, a:b] = z
                square = noise * noise
                for c in range(a, b, LANES):
                    cell = square[:, c - a:c - a + LANES]
                    if (steps - 1) * width + c + LANES > valid:
                        cell = jnp.where(jnp.concatenate([inside[:, c:c + LANES]] * 2, axis=0), cell, 0.0)
                    total = cell if total is None else total + cell
            sq_ref[row:row + samples] += total

    @pl.when(step == last)
    def _():
        for part in range(parts):
            multiply(groups - 1, part, held_b, w_now, step)
        sums[...] = jnp.zeros_like(sums)
        source = jnp.sum(src_ref[...].T, axis=0, keepdims=True) / math.sqrt(D)
        for block in range(rows // LANES):
            square = jnp.sum(sq_ref[block * LANES:(block + 1) * LANES].T, axis=0, keepdims=True)
            for at, left in ((0, square / NOISE_SCALE**2), (LANES, source)):
                sums[block * 16:block * 16 + 3, at:at + left.shape[1]] = three_terms(left)
        per = near_ref.shape[1] - 16
        outer = near_ref.shape[0]
        for other, ref in enumerate((near_ref, far_ref)):
            for shift in range(outer):
                to = lax.rem(lax.div(base_ref[1], 2) + shift, outer) * 2 + (base_ref[1] + other) % 2
                ref[shift, :per] = acc[pl.ds(pl.multiple_of(to * per, per), per), :].astype(ref.dtype)
                ref[shift, per:] = jnp.zeros((16, ref.shape[2]), ref.dtype)
                block = lax.div(to * per, LANES)
                ref[shift, per:, :2 * LANES] = sums[pl.ds(pl.multiple_of(block * 16, 16), 16), :].astype(ref.dtype)


def three_terms(left):
    terms = []
    for _ in range(3):
        terms.append(left.astype(jnp.bfloat16).astype(jnp.float32))
        left = left - terms[-1]
    return jnp.concatenate(terms, axis=0)


def combine_kernel(near_ref, got_ref, _, *out_refs):
    per = near_ref.shape[1] - 16
    for shift, ref in enumerate(out_refs):
        both = near_ref[shift].astype(jnp.float32) + got_ref[shift].astype(jnp.float32)
        ref[:per] = both[:per].astype(ref.dtype)
        terms = three_terms(jnp.sum(both[per:per + 3, :2 * LANES], axis=0, keepdims=True))
        ref[per:] = jnp.zeros((16, ref.shape[1]), ref.dtype)
        ref[per:, :2 * LANES] = jnp.concatenate([terms, jnp.zeros((13, 2 * LANES), jnp.float32)], axis=0).astype(ref.dtype)


def stack_kernel(_, *refs):
    *in_refs, out_ref, mark_ref = refs
    mark_ref[...] = jnp.zeros_like(mark_ref)
    for number, ref in enumerate(in_refs):
        out_ref[number] = ref[...]


def redraw_kernel(first, base_ref, pert_ref, point_ref, *refs):
    z_ref, mark_ref, keys, xs = refs[-4:]
    step = pl.program_id(0) + first
    rows, width = z_ref.shape
    points = point_ref.shape[0]
    samples = rows // points
    _, (key_zero, key_one, key_two) = column_keys(base_ref[0], step, width)
    keys[0:8] = key_zero
    keys[8:16] = key_one
    mark_ref[...] = jnp.zeros_like(mark_ref)
    for at in range(0, points, 8):
        xs[at:at + 8] = coordinate(point_rows(point_ref[at:at + 8], key_two, width))

    @pl.loop(0, points // 8)
    def _(block):
        eight = xs[pl.ds(pl.multiple_of(block * 8, 8), 8)]
        for inner in range(8):
            row = pl.multiple_of((block * 8 + inner) * samples, samples)
            seeds = pert_ref[pl.ds(row, samples)]
            for a, b in pieces(width):
                noise = draw(seeds, keys[0:8, a:b], keys[8:16, a:b])
                x = jnp.broadcast_to(eight[inner:inner + 1, a:b], (samples, b - a))
                z_ref[pl.ds(row, samples), a:b] = (x + noise).astype(jnp.bfloat16)


def gradient_kernel(count, places, base_ref, _, *refs):
    d_refs, refs = refs[:len(places)], refs[len(places):]
    blocks = len(places)
    z_refs, (keep_ref, send_ref, left) = refs[:count], refs[count:]
    half = keep_ref.shape[1]

    @pl.when(pl.program_id(0) == 0)
    def _():
        outer = blocks // 2
        for (other, shift), ref in zip(places, d_refs):
            block = lax.rem(lax.div(base_ref[1], 2) + outer - shift, outer) * 2 + (base_ref[1] + other) % 2
            for source in range(count):
                at = pl.multiple_of((source * blocks + block) * LANES, LANES)
                left[:, pl.ds(at, LANES)] = ref[source * LANES:(source + 1) * LANES, :].T

    width = keep_ref.shape[0]
    stride = 256 if width % 256 == 0 else LANES
    for a in range(0, width, stride):
        z = jnp.concatenate([ref[:, a:a + stride] for ref in z_refs], axis=0)
        part = jnp.dot(left[...], z, preferred_element_type=jnp.float32).astype(jnp.bfloat16).T
        keep_ref[a:a + stride, :] = part[:, :half]
        send_ref[a:a + stride, :] = part[:, half:]


def join_kernel(*refs):
    keep_ref, got_ref, out_ref = refs[0], refs[1], refs[-1]
    out_ref[...] = (keep_ref[...].astype(jnp.float32) + got_ref[...].astype(jnp.float32)).astype(jnp.bfloat16)


def params():
    return pltpu.CompilerParams(dimension_semantics=("arbitrary",), vmem_limit_bytes=VMEM_BYTES)


def whole(shape):
    return pl.BlockSpec(shape, lambda s: (0,) * len(shape))


def lanes_of(seeds):
    return jnp.broadcast_to(shuffle_bits(seeds.reshape(-1))[:, None], (seeds.size, LANES))


def forward(base, pert, point, coef, w, width, parts):
    valid, hidden = w.shape
    rows, points = pert.shape[0], point.shape[0]
    steps = -(-valid // width)
    smem = pl.BlockSpec(memory_space=pltpu.SMEM)
    return pl.pallas_call(
        functools.partial(forward_kernel, valid),
        grid=(steps,),
        in_specs=[
            smem, whole(pert.shape), whole(point.shape),
            pl.BlockSpec((1, width), lambda s: (0, s)),
            pl.BlockSpec((width, hidden), lambda s: (jnp.maximum(s - 1, 0), 0)),
            pl.BlockSpec((width, hidden), lambda s: (s, 0)),
        ],
        out_specs=[
            pl.BlockSpec((rows, width), lambda s: (0, s)),
        ] + [whole((parts // 2, rows // parts + 16, hidden))] * 2,
        out_shape=[
            jax.ShapeDtypeStruct((rows, steps * width), jnp.bfloat16),
        ] + [jax.ShapeDtypeStruct((parts // 2, rows // parts + 16, hidden), jnp.bfloat16)] * 2,
        scratch_shapes=[
            pltpu.VMEM((GROUP, width), jnp.bfloat16),
            pltpu.VMEM((GROUP, width), jnp.bfloat16),
            pltpu.VMEM((rows, hidden), jnp.float32),
            pltpu.VMEM((16, width), jnp.int32),
            pltpu.VMEM((points, width), jnp.float32),
            pltpu.VMEM((rows, LANES), jnp.float32),
            pltpu.VMEM((points, LANES), jnp.float32),
            pltpu.VMEM((rows // LANES * 16, 2 * LANES), jnp.float32),
        ],
        compiler_params=params(),
        cost_estimate=pl.CostEstimate(
            flops=100 * rows * valid * 40, bytes_accessed=4 * rows * valid, transcendentals=2 * rows * valid
        ),
        name="forward",
    )(base, pert, point, coef, w, w)


def redraw(base, pert, point, after, before, width, first, count, start, total):
    rows, points = pert.shape[0], point.shape[0]
    anywhere = pl.BlockSpec(memory_space=pl.ANY)
    extra = [] if before is None else [before]
    return pl.pallas_call(
        functools.partial(redraw_kernel, first),
        grid=(count,),
        in_specs=[pl.BlockSpec(memory_space=pltpu.SMEM), whole(pert.shape), whole(point.shape), anywhere]
        + [anywhere] * len(extra),
        out_specs=[pl.BlockSpec((rows, width), lambda s: (0, s + first - start)), whole((8, LANES))],
        out_shape=[
            jax.ShapeDtypeStruct((rows, total * width), jnp.bfloat16),
            jax.ShapeDtypeStruct((8, LANES), jnp.float32),
        ],
        input_output_aliases={4: 0} if extra else {},
        scratch_shapes=[pltpu.VMEM((16, width), jnp.int32), pltpu.VMEM((points, width), jnp.float32)],
        compiler_params=params(),
        cost_estimate=pl.CostEstimate(
            flops=100 * rows * width * count * 40, bytes_accessed=2 * rows * width * count,
            transcendentals=2 * rows * width * count,
        ),
        name="redraw",
    )(base, pert, point, after, *extra)


def combine(near, got, after):
    parts, rows, hidden = near.shape
    return pl.pallas_call(
        combine_kernel,
        grid=(1,),
        in_specs=[whole(near.shape)] * 2 + [pl.BlockSpec(memory_space=pl.ANY)],
        out_specs=[whole((rows, hidden))] * parts,
        out_shape=[jax.ShapeDtypeStruct((rows, hidden), jnp.bfloat16)] * parts,
        compiler_params=params(),
        cost_estimate=pl.CostEstimate(flops=parts * rows * hidden, bytes_accessed=6 * parts * rows * hidden, transcendentals=0),
        name="combine",
    )(near, got, after)


def stack(after, *arrays):
    shape = arrays[0].shape
    return pl.pallas_call(
        stack_kernel,
        grid=(1,),
        in_specs=[pl.BlockSpec(memory_space=pl.ANY)] + [whole(shape)] * len(arrays),
        out_specs=[whole((len(arrays), *shape)), whole((8, LANES))],
        out_shape=[
            jax.ShapeDtypeStruct((len(arrays), *shape), arrays[0].dtype),
            jax.ShapeDtypeStruct((8, LANES), jnp.float32),
        ],
        compiler_params=params(),
        cost_estimate=pl.CostEstimate(flops=0, bytes_accessed=4 * len(arrays) * math.prod(shape), transcendentals=0),
        name="stack",
    )(after, *arrays)


def gradient(base, after, cotangent, places, own, others, width, first, count, valid):
    if count % 2 == 0 and first % 2 == 0:
        width, first, count = 2 * width, first // 2, count // 2
    rows = own.shape[0]
    half = cotangent[0].shape[1] // 2
    height = min(valid, (first + count) * width) - first * width
    return pl.pallas_call(
        functools.partial(gradient_kernel, 1 + len(others), places),
        grid=(count,),
        in_specs=[pl.BlockSpec(memory_space=pltpu.SMEM), pl.BlockSpec(memory_space=pl.ANY)]
        + [whole(part.shape) for part in cotangent]
        + [pl.BlockSpec((rows, width), lambda s: (0, s + first))]
        + [pl.BlockSpec((rows, width), lambda s: (0, s)) for _ in others],
        out_specs=[pl.BlockSpec((width, half), lambda s: (s, 0))] * 2,
        out_shape=[jax.ShapeDtypeStruct((height, half), jnp.bfloat16)] * 2,
        scratch_shapes=[pltpu.VMEM((2 * half, (1 + len(others)) * rows), jnp.bfloat16)],
        compiler_params=params(),
        cost_estimate=pl.CostEstimate(
            flops=4 * half * rows * (1 + len(others)) * width * count,
            bytes_accessed=2 * rows * (1 + len(others)) * width * count, transcendentals=0,
        ),
        name="gradient",
    )(base, after, *cotangent, own, *others)


def join(keep, got, before, width, first, valid):
    height, half = keep.shape
    count = -(-height // width)
    specs = [pl.BlockSpec((width, half), lambda s: (s, 0))] * 2
    operands, aliases = [keep, got], {}
    if before is not None:
        specs, operands, aliases = specs + [pl.BlockSpec(memory_space=pl.ANY)], operands + [before], {2: 0}
    return pl.pallas_call(
        join_kernel,
        grid=(count,),
        in_specs=specs,
        out_specs=pl.BlockSpec((width, half), lambda s: (s + first, 0)),
        out_shape=jax.ShapeDtypeStruct((valid, half), jnp.bfloat16),
        input_output_aliases=aliases,
        compiler_params=params(),
        cost_estimate=pl.CostEstimate(flops=height * half, bytes_accessed=6 * height * half, transcendentals=0),
        name="join",
    )(*operands)


def hidden_pass(pre_first, squares, source, w2, w3, count_samples):
    hidden_one = jnp.tanh(pre_first).astype(jnp.bfloat16)
    pre_second = lax.dot_general(
        hidden_one, w2, (((1,), (1,)), ((), ())), preferred_element_type=jnp.float32
    )
    hidden_two = jnp.tanh(pre_second).astype(jnp.bfloat16)
    values_out = READOUT * jnp.dot(hidden_two, w3, preferred_element_type=jnp.float32)
    stein_weight = (squares - D) / (NOISE_SCALE * NOISE_SCALE * count_samples)
    per_point = (stein_weight * values_out).reshape(-1, count_samples)
    residual = jnp.sum(per_point, axis=1) - source
    grad_values = (residual[:, None] * stein_weight.reshape(-1, count_samples)).reshape(-1)
    two_float = hidden_two.astype(jnp.float32)
    grad_readout = READOUT * jnp.sum(grad_values[:, None] * two_float, axis=0)
    grad_pre_two = (
        READOUT
        * grad_values[:, None]
        * w3.astype(jnp.float32)[None, :]
        * (1.0 - two_float * two_float)
    ).astype(jnp.bfloat16)
    grad_hidden = jnp.dot(grad_pre_two, w2, preferred_element_type=jnp.float32)
    one_float = hidden_one.astype(jnp.float32)
    grad_pre_one = (grad_hidden * (1.0 - one_float * one_float)).astype(jnp.bfloat16)
    return (residual, grad_pre_one, grad_readout, hidden_one, grad_pre_two)


def block_width(valid):
    tiles = -(-valid // LANES)
    best = min((8, 7, 6, 5), key=lambda t: -(-tiles // t) * t)
    return best * LANES


def shards(point_seed, pert_seed, source_coef, w1, b1, w2, w3):
    coord_count = lax.axis_size("coord")
    pts_count = lax.axis_size("pts")
    chips = pts_count // 2
    hidden, valid = w1.shape
    points_here, samples = pert_seed.shape
    rows_here = points_here * samples
    rows_local = rows_here // coord_count
    points_local = points_here // coord_count
    coord_index = lax.axis_index("coord")
    pts_index = lax.axis_index("pts")
    share = hidden // pts_count
    width = block_width(valid)
    steps = -(-valid // width)
    base = jnp.stack([coord_index * valid, coord_index]).astype(jnp.int32)

    def shift(a, by):
        return jax.tree.map(
            lambda leaf: lax.ppermute(
                leaf, "pts", [(i, (i + 2 * by) % pts_count) for i in range(pts_count)]
            ), a,
        )

    other_seeds = [shift((pert_seed, point_seed), by) for by in range(1, chips)]

    pert, point = lanes_of(pert_seed), lanes_of(point_seed)
    own, near, far = forward(base, pert, point, source_coef[None, :], w1.T, width, coord_count)
    others_in = [(lanes_of(a), lanes_of(b)) for a, b in other_seeds]
    outer = coord_count // 2

    def across(a):
        return lax.ppermute(a, "coord", [(i, i ^ 1) for i in range(coord_count)])

    def along(a, by):
        return lax.ppermute(a, "coord", [(i, (i + 2 * by) % coord_count) for i in range(coord_count)])

    early = steps // 2 + (steps // 2) % 2
    cuts = [(0, early), (early, steps - early)]

    def redraws(number, after):
        first, count = cuts[number]
        held = [None] * len(others_in)
        for at, size in ((0, -(-count // 2)), (-(-count // 2), count // 2)):
            made = [
                redraw(base, a, b, after, z, width, first + at, size, first, count)
                for (a, b), z in zip(others_in, held)
            ]
            held = [z for z, _ in made]
            after = yield held, sum(mark for _, mark in made)

    draws = redraws(0, near)
    _, mark = next(draws)
    parts = combine(near, across(far), mark)
    drawn_first, mark = draws.send(parts[0])
    total = parts[0].astype(jnp.float32)
    for by in range(1, outer):
        total += along(parts[by], by).astype(jnp.float32)
    pre_local = total[:rows_local]
    sums = jnp.sum(total[rows_local:rows_local + 3], axis=0)
    squares_local = lax.dynamic_slice_in_dim(sums, coord_index * rows_local % LANES, rows_local, 0)
    source_local = lax.dynamic_slice_in_dim(sums, LANES + coord_index * points_local, points_local, 0)
    b1 = b1 + mark[0, 0]
    residual, grad_pre_one, grad_readout, hidden_one, grad_pre_two = hidden_pass(
        pre_local.astype(jnp.float32) + b1[None, :], squares_local, source_local, w2, w3, samples
    )

    def share_of(index):
        return jnp.concatenate(
            [lax.dynamic_slice_in_dim(grad_pre_one, i * share, share, 1) for i in (index, index ^ 1)], axis=1
        )

    sent = [share_of((pts_index + 2 * by) % pts_count) for by in range(chips)]
    readout_rows = grad_readout.astype(jnp.bfloat16).reshape(-1, 2 * share)
    readout_rows = jnp.pad(readout_rows, ((0, 16 - readout_rows.shape[0]), (0, 0)))
    mine = jnp.concatenate([sent[0]] + [shift(sent[by], by) for by in range(1, chips)] + [readout_rows], axis=0)
    draws = redraws(1, mine)
    _, mark = next(draws)
    if rows_local == LANES:
        cotangent = [mine] + [along(mine, by) for by in range(1, outer)] + [across(mine)]
        got, mark = stack(mark, *cotangent[1:outer])
        got = across(got)
        cotangent += [got[i] for i in range(outer - 1)]
        places = [(other, shift) for other in range(2) for shift in range(outer)]
        turn = base
    else:
        gathered = lax.all_gather(mine, "coord", axis=0)
        cotangent = [gathered[i] for i in range(coord_count)]
        turn = jnp.zeros_like(base)
    drawn_second, _ = draws.send(mark)
    drawn = [drawn_first, drawn_second]

    def rotate(a, by):
        return lax.ppermute(a, "pts", [(i, (i + by) % pts_count) for i in range(pts_count)])

    grad_second = lax.dot_general(
        grad_pre_two, hidden_one, (((0,), (0,)), ((), ())), preferred_element_type=jnp.float32
    )
    grad_second = (grad_second + mark[0, 0]).astype(jnp.bfloat16)
    quarter = hidden // coord_count // pts_count
    grad_second = grad_second.reshape(coord_count, pts_count, quarter, hidden)

    def second_part(index):
        return lax.dynamic_slice_in_dim(grad_second, index, 1, 1).reshape(coord_count * quarter, hidden)

    second = second_part(pts_index).astype(jnp.float32)
    for by in range(1, pts_count):
        second += rotate(second_part((pts_index + by) % pts_count), by).astype(jnp.float32)
    scattered = lax.psum_scatter(second.astype(jnp.bfloat16), "coord", scatter_dimension=0, tiled=True)
    second = lax.all_gather(scattered, "pts", axis=0, tiled=True).astype(jnp.float32)

    summed = sum(part.astype(jnp.float32) for part in cotangent)
    bias_half = jnp.sum(summed[:chips * rows_local], axis=0)
    readout = summed[chips * rows_local:chips * rows_local + pts_count // 2].reshape(-1)
    bias = jnp.zeros((hidden,), jnp.float32)
    for number, index in enumerate((pts_index, pts_index ^ 1)):
        bias = lax.dynamic_update_slice_in_dim(bias, bias_half[number * share:(number + 1) * share], index * share, 0)
    vectors = jnp.stack([bias, readout]).reshape(-1, LANES)
    vectors = vectors + sum(rotate(vectors, by) for by in range(1, pts_count))
    bias, readout = (
        lax.dynamic_slice_in_dim(v, coord_index * (hidden // coord_count), hidden // coord_count, 0)
        for v in vectors.reshape(2, hidden)
    )

    if rows_local != LANES:
        rows = jnp.stack(cotangent)[:, :chips * rows_local].reshape(coord_count, chips, rows_local, -1)
        rows = rows.transpose(1, 0, 2, 3).reshape(chips, -1, LANES, 2 * share).transpose(1, 0, 2, 3)
        rows = rows.reshape(-1, chips * LANES, 2 * share)
        cotangent = [rows[i] for i in range(rows.shape[0])]
        places = [(i % 2, -(i // 2) % (len(cotangent) // 2)) for i in range(len(cotangent))]

    out = None
    swap = [(i, i ^ 1) for i in range(pts_count)]
    for (first, count), z, after in zip(cuts, drawn, (mine, mine)):
        keep, send = gradient(turn, after, cotangent, places, own, z, width, first, count, valid)
        got = lax.ppermute(send, "pts", swap)
        wide = 2 * width if count % 2 == 0 and first % 2 == 0 else width
        out = join(keep, got, out, wide, first * width // wide, valid)
    return (residual, out.T, second, bias, readout)


def solution(mesh):
    return jax.shard_map(
        shards,
        mesh=mesh,
        in_specs=(P("pts"), P("pts", None), P("coord"), P(None, "coord"), P(), P(), P()),
        out_specs=(
            P(("pts", "coord")),
            P("pts", "coord"),
            P("coord", None),
            P("coord"),
            P("coord"),
        ),
        check_vma=False,
    )
```

```python
import functools
import math

import jax
import jax.numpy as jnp
import numpy as np
from jax import lax
from jax.experimental import pallas as pl
from jax.experimental.pallas import tpu as pltpu
from jax.sharding import PartitionSpec as P

D = 100000

HASH_FACTOR = 73244475
NOISE_SCALE = 2.0
READOUT = 0.0625
LANES = 128
GROUP = 256
MASK = 8388607
VMEM_BYTES = 56 * 1024 * 1024

C0, C1, C2, C3 = 6.283164044286755, -2.583571398038591, 0.3177373780982648, -0.017332380925367475
B0, B1, B2 = C0 / C3, C1 / C3, C2 / C3
SINE_SCALE = -C3 * 2.0**-23
LOG_SCALE = -2.0 * (NOISE_SCALE * SINE_SCALE) ** 2


def shuffle_bits(bits):
    return bits ^ lax.shift_right_logical(bits, jnp.full_like(bits, 16))


def mix_tail(bits):
    bits = shuffle_bits(bits * HASH_FACTOR)
    return shuffle_bits(bits * HASH_FACTOR)


def mix_bits(bits):
    return mix_tail(shuffle_bits(bits))


def turn_wave(index):
    y = 2097152.0 - jnp.abs(index.astype(jnp.float32) + (0.5 - 4194304.0))
    s = (y * y) * 2.0**-42
    m = ((s + B2) * s + B1) * s + B0
    return y, m


def spread_seeds(seeds_ref, point_ref, pert, point):
    samples, points = seeds_ref.shape
    seeds = shuffle_bits(seeds_ref[...])
    for number in range(points):
        pert[number * samples:(number + 1) * samples] = jnp.broadcast_to(seeds[:, number:number + 1], (samples, LANES))
    point[...] = jnp.broadcast_to(shuffle_bits(point_ref[...]), (LANES, points)).T


def tile_lanes(a, width):
    return jnp.concatenate([a] * (width // a.shape[1]), axis=1)


def column_keys(base, step, width):
    columns = lax.broadcasted_iota(jnp.int32, (8, width), 1) + step * width
    four = (columns + base) * 4
    return columns, [shuffle_bits(mix_bits(four + t)) for t in range(3)]


def draw(seeds, key_zero, key_one):
    width = key_zero.shape[1]
    seeds = tile_lanes(seeds, width)
    first = mix_tail(seeds ^ jnp.concatenate([key_zero] * 2, axis=0))
    second = mix_tail(seeds ^ jnp.concatenate([key_one] * 2, axis=0))
    u0 = ((first & MASK).astype(jnp.float32) + 0.5) * 2.0**-23
    n = jnp.log(u0) * LOG_SCALE
    y, m = turn_wave(second & MASK)
    return ((n * lax.rsqrt(n)) * y) * m


def pieces(width):
    tiles = width // LANES
    parts = -(-tiles // 2)
    edges = [tiles * i // parts for i in range(parts + 1)]
    return [(a * LANES, b * LANES) for a, b in zip(edges, edges[1:])]


def point_rows(seeds, key, width):
    return mix_tail(tile_lanes(seeds, width) ^ key) & MASK


def coordinate(index):
    return (index.astype(jnp.float32) + (0.5 - 4194304.0)) * 2.0**-22


def forward_kernel(
    valid, base_ref, seeds_ref, spots_ref, coef_ref, w_prev, w_now, z_ref, *refs,
):
    near_ref, far_ref, held_a, held_b, acc, keys, xs, sq_ref, src_ref, sums, pert_ref, point_ref = refs
    step, last = pl.program_id(0), pl.num_programs(0) - 1
    rows, width = z_ref.shape
    points = point_ref.shape[0]
    samples = rows // points
    groups = rows // GROUP
    steps = -(-valid // width)
    pad = steps * width - valid

    @pl.when(step == 0)
    def _():
        acc[...] = jnp.zeros_like(acc)
        held_b[...] = jnp.zeros_like(held_b)
        sq_ref[...] = jnp.zeros_like(sq_ref)
        src_ref[...] = jnp.zeros_like(src_ref)
        spread_seeds(seeds_ref, spots_ref, pert_ref, point_ref)

    columns, (key_zero, key_one, key_two) = column_keys(base_ref[0], step, width)
    keys[0:8] = key_zero
    keys[8:16] = key_one
    inside = columns < valid
    coef = jnp.where(inside, jnp.broadcast_to(coef_ref[...], (8, width)), 0.0)
    for at in range(0, points, 8):
        index = point_rows(point_ref[at:at + 8], key_two, width)
        xs[at:at + 8] = coordinate(index)
        y, m = turn_wave((index + 2097152) & MASK)
        term = ((y * SINE_SCALE) * m) * coef
        src_ref[at:at + 8] += sum(
            term[:, a:a + LANES] for a in range(0, width, LANES)
        )

    cut = width - -(-pad // 16) * 16

    def multiply(group, part, held, ref, of):
        at, left = group * GROUP, part * GROUP
        w = ref[:, left:left + GROUP]
        if pad:
            place = lax.broadcasted_iota(jnp.int32, (width - cut, GROUP), 0) + (of * width + cut)
            tail = jnp.where(place < valid, w[cut:], jnp.zeros((), w.dtype))
            w = jnp.concatenate([w[:cut], tail], axis=0)
        acc[at:at + GROUP, left:left + GROUP] += jnp.dot(
            held[...], w, preferred_element_type=jnp.float32
        )

    parts = acc.shape[1] // GROUP
    group_points = GROUP // samples

    for group in range(groups):
        held = (held_a, held_b)[group % 2]
        other = (held_b, held_a)[group % 2]
        for number in range(group_points):
            if number % (group_points // parts) == 0:
                part = number // (group_points // parts)
                if group == 0:
                    multiply(groups - 1, part, other, w_prev, jnp.maximum(step - 1, 0))
                else:
                    multiply(group - 1, part, other, w_now, step)
            at = number * samples
            row = group * GROUP + at
            point = row // samples
            seeds = pert_ref[row:row + samples]
            total = None
            for a, b in pieces(width):
                noise = draw(seeds, keys[0:8, a:b], keys[8:16, a:b])
                x = jnp.broadcast_to(xs[point:point + 1, a:b], (samples, b - a))
                z = (x + noise).astype(jnp.bfloat16)
                held[at:at + samples, a:b] = z
                z_ref[row:row + samples, a:b] = z
                square = noise * noise
                for c in range(a, b, LANES):
                    cell = square[:, c - a:c - a + LANES]
                    if (steps - 1) * width + c + LANES > valid:
                        cell = jnp.where(jnp.concatenate([inside[:, c:c + LANES]] * 2, axis=0), cell, 0.0)
                    total = cell if total is None else total + cell
            sq_ref[row:row + samples] += total

    @pl.when(step == last)
    def _():
        for part in range(parts):
            multiply(groups - 1, part, held_b, w_now, step)
        sums[...] = jnp.zeros_like(sums)
        source = jnp.sum(src_ref[...].T, axis=0, keepdims=True) / math.sqrt(D)
        for block in range(rows // LANES):
            square = jnp.sum(sq_ref[block * LANES:(block + 1) * LANES].T, axis=0, keepdims=True)
            for at, left in ((0, square / NOISE_SCALE**2), (LANES, source)):
                sums[block * 16:block * 16 + 3, at:at + left.shape[1]] = three_terms(left)
        per = near_ref.shape[1] - 16
        outer = near_ref.shape[0]
        for other, ref in enumerate((near_ref, far_ref)):
            for shift in range(outer):
                to = lax.rem(lax.div(base_ref[1], 2) + shift, outer) * 2 + (base_ref[1] + other) % 2
                ref[shift, :per] = acc[pl.ds(pl.multiple_of(to * per, per), per), :].astype(ref.dtype)
                ref[shift, per:] = jnp.zeros((16, ref.shape[2]), ref.dtype)
                block = lax.div(to * per, LANES)
                ref[shift, per:, :2 * LANES] = sums[pl.ds(pl.multiple_of(block * 16, 16), 16), :].astype(ref.dtype)


def three_terms(left):
    terms = []
    for _ in range(3):
        terms.append(left.astype(jnp.bfloat16).astype(jnp.float32))
        left = left - terms[-1]
    return jnp.concatenate(terms, axis=0)


def combine_kernel(near_ref, got_ref, _, *out_refs):
    per = near_ref.shape[1] - 16
    for shift, ref in enumerate(out_refs):
        both = near_ref[shift].astype(jnp.float32) + got_ref[shift].astype(jnp.float32)
        ref[:per] = both[:per].astype(ref.dtype)
        terms = three_terms(jnp.sum(both[per:per + 3, :2 * LANES], axis=0, keepdims=True))
        ref[per:] = jnp.zeros((16, ref.shape[1]), ref.dtype)
        ref[per:, :2 * LANES] = jnp.concatenate([terms, jnp.zeros((13, 2 * LANES), jnp.float32)], axis=0).astype(ref.dtype)


def stack_kernel(_, *refs):
    *in_refs, out_ref, mark_ref = refs
    mark_ref[...] = jnp.zeros_like(mark_ref)
    for number, ref in enumerate(in_refs):
        out_ref[number] = ref[...]


def redraw_kernel(first, base_ref, seeds_ref, spots_ref, *refs):
    z_ref, mark_ref, keys, xs, pert_ref, point_ref = refs[-6:]

    @pl.when(pl.program_id(0) == 0)
    def _():
        spread_seeds(seeds_ref, spots_ref, pert_ref, point_ref)

    step = pl.program_id(0) + first
    rows, width = z_ref.shape
    points = point_ref.shape[0]
    samples = rows // points
    _, (key_zero, key_one, key_two) = column_keys(base_ref[0], step, width)
    keys[0:8] = key_zero
    keys[8:16] = key_one
    mark_ref[...] = jnp.zeros_like(mark_ref)
    for at in range(0, points, 8):
        xs[at:at + 8] = coordinate(point_rows(point_ref[at:at + 8], key_two, width))

    @pl.loop(0, points // 8)
    def _(block):
        eight = xs[pl.ds(pl.multiple_of(block * 8, 8), 8)]
        for inner in range(8):
            row = pl.multiple_of((block * 8 + inner) * samples, samples)
            seeds = pert_ref[pl.ds(row, samples)]
            for a, b in pieces(width):
                noise = draw(seeds, keys[0:8, a:b], keys[8:16, a:b])
                x = jnp.broadcast_to(eight[inner:inner + 1, a:b], (samples, b - a))
                z_ref[pl.ds(row, samples), a:b] = (x + noise).astype(jnp.bfloat16)


def gradient_kernel(count, places, skip, joins, base_ref, *refs):
    refs = refs[skip:]
    if joins:
        keep, got, *refs, out_ref, left = refs
        out_ref[...] = (keep[...].astype(jnp.float32) + got[...].astype(jnp.float32)).astype(jnp.bfloat16)
        refs = [*refs, left]
    d_refs, refs = refs[:len(places)], refs[len(places):]
    blocks = len(places)
    z_refs, (keep_ref, send_ref, left) = refs[:count], refs[count:]
    half = keep_ref.shape[1]

    @pl.when(pl.program_id(0) == 0)
    def _():
        outer = blocks // 2
        for (other, shift), ref in zip(places, d_refs):
            block = lax.rem(lax.div(base_ref[1], 2) + outer - shift, outer) * 2 + (base_ref[1] + other) % 2
            for source in range(count):
                at = pl.multiple_of((source * blocks + block) * LANES, LANES)
                left[:, pl.ds(at, LANES)] = ref[source * LANES:(source + 1) * LANES, :].T

    width = keep_ref.shape[0]
    for a in range(0, width, 1024):
        b = min(a + 1024, width)
        z = jnp.concatenate([ref[:, a:b] for ref in z_refs], axis=0)
        part = jnp.dot(left[...], z, preferred_element_type=jnp.float32).astype(jnp.bfloat16).T
        keep_ref[a:b, :] = part[:, :half]
        send_ref[a:b, :] = part[:, half:]


def join_kernel(*refs):
    keep_ref, got_ref, out_ref = refs[0], refs[1], refs[-1]
    out_ref[...] = (keep_ref[...].astype(jnp.float32) + got_ref[...].astype(jnp.float32)).astype(jnp.bfloat16)


def params():
    return pltpu.CompilerParams(dimension_semantics=("arbitrary",), vmem_limit_bytes=VMEM_BYTES)


def whole(shape):
    return pl.BlockSpec(shape, lambda s: (0,) * len(shape))


def forward(base, pert, point, coef, w, width, parts):
    valid, hidden = w.shape
    rows, points = pert.size, point.size
    steps = -(-valid // width)
    smem = pl.BlockSpec(memory_space=pltpu.SMEM)
    return pl.pallas_call(
        functools.partial(forward_kernel, valid),
        grid=(steps,),
        in_specs=[
            smem, whole(pert.shape), whole(point.shape),
            pl.BlockSpec((1, width), lambda s: (0, s)),
            pl.BlockSpec((width, hidden), lambda s: (jnp.maximum(s - 1, 0), 0)),
            pl.BlockSpec((width, hidden), lambda s: (s, 0)),
        ],
        out_specs=[
            pl.BlockSpec((rows, width), lambda s: (0, s)),
        ] + [whole((parts // 2, rows // parts + 16, hidden))] * 2,
        out_shape=[
            jax.ShapeDtypeStruct((rows, steps * width), jnp.bfloat16),
        ] + [jax.ShapeDtypeStruct((parts // 2, rows // parts + 16, hidden), jnp.bfloat16)] * 2,
        scratch_shapes=[
            pltpu.VMEM((GROUP, width), jnp.bfloat16),
            pltpu.VMEM((GROUP, width), jnp.bfloat16),
            pltpu.VMEM((rows, hidden), jnp.float32),
            pltpu.VMEM((16, width), jnp.int32),
            pltpu.VMEM((points, width), jnp.float32),
            pltpu.VMEM((rows, LANES), jnp.float32),
            pltpu.VMEM((points, LANES), jnp.float32),
            pltpu.VMEM((rows // LANES * 16, 2 * LANES), jnp.float32),
            pltpu.VMEM((rows, LANES), jnp.int32),
            pltpu.VMEM((points, LANES), jnp.int32),
        ],
        compiler_params=params(),
        cost_estimate=pl.CostEstimate(
            flops=100 * rows * valid * 40, bytes_accessed=4 * rows * valid, transcendentals=2 * rows * valid
        ),
        name="forward",
    )(base, pert, point, coef, w, w)


def redraw(base, pert, point, after, before, width, first, count, start, total):
    rows, points = pert.size, point.size
    anywhere = pl.BlockSpec(memory_space=pl.ANY)
    extra = [] if before is None else [before]
    return pl.pallas_call(
        functools.partial(redraw_kernel, first),
        grid=(count,),
        in_specs=[pl.BlockSpec(memory_space=pltpu.SMEM), whole(pert.shape), whole(point.shape)]
        + [anywhere] * (len(after) + len(extra)),
        out_specs=[pl.BlockSpec((rows, width), lambda s: (0, s + first - start)), whole((8, LANES))],
        out_shape=[
            jax.ShapeDtypeStruct((rows, total * width), jnp.bfloat16),
            jax.ShapeDtypeStruct((8, LANES), jnp.float32),
        ],
        input_output_aliases={3 + len(after): 0} if extra else {},
        scratch_shapes=[
            pltpu.VMEM((16, width), jnp.int32), pltpu.VMEM((points, width), jnp.float32),
            pltpu.VMEM((rows, LANES), jnp.int32), pltpu.VMEM((points, LANES), jnp.int32),
        ],
        compiler_params=params(),
        cost_estimate=pl.CostEstimate(
            flops=100 * rows * width * count * 40, bytes_accessed=2 * rows * width * count,
            transcendentals=2 * rows * width * count,
        ),
        name="redraw",
    )(base, pert, point, *after, *extra)


def combine(near, got, after):
    parts, rows, hidden = near.shape
    return pl.pallas_call(
        combine_kernel,
        grid=(1,),
        in_specs=[whole(near.shape)] * 2 + [pl.BlockSpec(memory_space=pl.ANY)],
        out_specs=[whole((rows, hidden))] * parts,
        out_shape=[jax.ShapeDtypeStruct((rows, hidden), jnp.bfloat16)] * parts,
        compiler_params=params(),
        cost_estimate=pl.CostEstimate(flops=parts * rows * hidden, bytes_accessed=6 * parts * rows * hidden, transcendentals=0),
        name="combine",
    )(near, got, after)


def stack(after, *arrays):
    shape = arrays[0].shape
    return pl.pallas_call(
        stack_kernel,
        grid=(1,),
        in_specs=[pl.BlockSpec(memory_space=pl.ANY)] + [whole(shape)] * len(arrays),
        out_specs=[whole((len(arrays), *shape)), whole((8, LANES))],
        out_shape=[
            jax.ShapeDtypeStruct((len(arrays), *shape), arrays[0].dtype),
            jax.ShapeDtypeStruct((8, LANES), jnp.float32),
        ],
        compiler_params=params(),
        cost_estimate=pl.CostEstimate(flops=0, bytes_accessed=4 * len(arrays) * math.prod(shape), transcendentals=0),
        name="stack",
    )(after, *arrays)


def gradient(base, after, cotangent, places, own, others, width, first, count, start, valid, joined=None):
    if all(n % 2 == 0 for n in (count, first, start)):
        width, first, count, start = 2 * width, first // 2, count // 2, start // 2
    rows = own.shape[0]
    half = cotangent[0].shape[1] // 2
    height = min(valid, (first + count) * width) - first * width
    out_specs = [pl.BlockSpec((width, half), lambda s: (s, 0))] * 2
    out_shape = [jax.ShapeDtypeStruct((height, half), jnp.bfloat16)] * 2
    joins, spec = [], None
    if joined is not None:
        joins = list(joined)
        spec = pl.BlockSpec((joins[0].shape[0] // count, half), lambda s: (s, 0))
        out_specs, out_shape = out_specs + [spec], out_shape + [jax.ShapeDtypeStruct((valid, half), jnp.bfloat16)]
    return pl.pallas_call(
        functools.partial(gradient_kernel, 1 + len(others), places, len(after), len(joins) > 0),
        grid=(count,),
        in_specs=[pl.BlockSpec(memory_space=pltpu.SMEM)] + [pl.BlockSpec(memory_space=pl.ANY)] * len(after)
        + [spec] * len(joins)
        + [whole(part.shape) for part in cotangent]
        + [pl.BlockSpec((rows, width), lambda s: (0, s + first))]
        + [pl.BlockSpec((rows, width), lambda s: (0, s + first - start)) for _ in others],
        out_specs=out_specs,
        out_shape=out_shape,
        scratch_shapes=[pltpu.VMEM((2 * half, (1 + len(others)) * rows), jnp.bfloat16)],
        compiler_params=params(),
        cost_estimate=pl.CostEstimate(
            flops=4 * half * rows * (1 + len(others)) * width * count,
            bytes_accessed=2 * rows * (1 + len(others)) * width * count, transcendentals=0,
        ),
        name="gradient",
    )(base, *after, *joins, *cotangent, own, *others)


def join(after, keep, got, before, width, first, valid):
    height, half = keep.shape
    count = -(-height // width)
    anywhere = pl.BlockSpec(memory_space=pl.ANY)
    specs = [pl.BlockSpec((width, half), lambda s: (s, 0))] * 2 + [anywhere] * len(after)
    operands, aliases = [keep, got, *after], {}
    if before is not None:
        specs, operands, aliases = specs + [anywhere], operands + [before], {len(operands): 0}
    return pl.pallas_call(
        join_kernel,
        grid=(count,),
        in_specs=specs,
        out_specs=pl.BlockSpec((width, half), lambda s: (s + first, 0)),
        out_shape=jax.ShapeDtypeStruct((valid, half), jnp.bfloat16),
        input_output_aliases=aliases,
        compiler_params=params(),
        cost_estimate=pl.CostEstimate(flops=height * half, bytes_accessed=6 * height * half, transcendentals=0),
        name="join",
    )(*operands)


def hidden_pass(pre_first, squares, source, w2, w3, count_samples):
    hidden_one = jnp.tanh(pre_first).astype(jnp.bfloat16)
    pre_second = lax.dot_general(
        hidden_one, w2, (((1,), (1,)), ((), ())), preferred_element_type=jnp.float32
    )
    hidden_two = jnp.tanh(pre_second).astype(jnp.bfloat16)
    values_out = READOUT * jnp.dot(hidden_two, w3, preferred_element_type=jnp.float32)
    stein_weight = (squares - D) / (NOISE_SCALE * NOISE_SCALE * count_samples)
    per_point = (stein_weight * values_out).reshape(-1, count_samples)
    residual = jnp.sum(per_point, axis=1) - source
    grad_values = (residual[:, None] * stein_weight.reshape(-1, count_samples)).reshape(-1)
    two_float = hidden_two.astype(jnp.float32)
    grad_readout = READOUT * jnp.sum(grad_values[:, None] * two_float, axis=0)
    grad_pre_two = (
        READOUT
        * grad_values[:, None]
        * w3.astype(jnp.float32)[None, :]
        * (1.0 - two_float * two_float)
    ).astype(jnp.bfloat16)
    grad_hidden = jnp.dot(grad_pre_two, w2, preferred_element_type=jnp.float32)
    one_float = hidden_one.astype(jnp.float32)
    grad_pre_one = (grad_hidden * (1.0 - one_float * one_float)).astype(jnp.bfloat16)
    return (residual, grad_pre_one, grad_readout, hidden_one, grad_pre_two)


def block_width(valid):
    tiles = -(-valid // LANES)
    best = min((8, 7, 6, 5), key=lambda t: -(-tiles // t) * t)
    return best * LANES


def shards(point_seed, pert_seed, source_coef, w1, b1, w2, w3):
    coord_count = lax.axis_size("coord")
    pts_count = lax.axis_size("pts")
    chips = pts_count // 2
    hidden, valid = w1.shape
    points_here, samples = pert_seed.shape
    rows_here = points_here * samples
    rows_local = rows_here // coord_count
    points_local = points_here // coord_count
    coord_index = lax.axis_index("coord")
    pts_index = lax.axis_index("pts")
    share = hidden // pts_count
    width = block_width(valid)
    steps = -(-valid // width)
    base = jnp.stack([coord_index * valid, coord_index]).astype(jnp.int32)

    def shift(a, by):
        return jax.tree.map(
            lambda leaf: lax.ppermute(
                leaf, "pts", [(i, (i + 2 * by) % pts_count) for i in range(pts_count)]
            ), a,
        )

    other_seeds = [shift((pert_seed, point_seed), by) for by in range(1, chips)]

    pert, point = pert_seed.T, point_seed[None, :]
    own, near, far = forward(base, pert, point, source_coef[None, :], w1.T, width, coord_count)
    others_in = [(a.T, b[None, :]) for a, b in other_seeds]
    outer = coord_count // 2

    def across(a):
        return lax.ppermute(a, "coord", [(i, i ^ 1) for i in range(coord_count)])

    def along(a, by):
        return lax.ppermute(a, "coord", [(i, (i + 2 * by) % coord_count) for i in range(coord_count)])

    early = steps // 2 + (steps // 2) % 2
    cuts = [(0, early), (early, steps - early)]

    def redraws(number, after):
        first, count = cuts[number]
        held = [None] * len(others_in)
        for at, size in ((0, -(-count // 2)), (-(-count // 2), count // 2)):
            made = [
                redraw(base, a, b, after, z, width, first + at, size, first, count)
                for (a, b), z in zip(others_in, held)
            ]
            held = [z for z, _ in made]
            after = yield held, sum(mark for _, mark in made)

    draws = redraws(0, [near])
    _, mark = next(draws)
    parts = combine(near, across(far), mark)
    drawn_first, mark = draws.send([parts[0]])
    total = parts[0].astype(jnp.float32)
    for by in range(1, outer):
        total += along(parts[by], by).astype(jnp.float32)
    pre_local = total[:rows_local]
    sums = jnp.sum(total[rows_local:rows_local + 3], axis=0)
    squares_local = lax.dynamic_slice_in_dim(sums, coord_index * rows_local % LANES, rows_local, 0)
    source_local = lax.dynamic_slice_in_dim(sums, LANES + coord_index * points_local, points_local, 0)
    b1 = b1 + mark[0, 0]
    residual, grad_pre_one, grad_readout, hidden_one, grad_pre_two = hidden_pass(
        pre_local.astype(jnp.float32) + b1[None, :], squares_local, source_local, w2, w3, samples
    )

    def share_of(index):
        return jnp.concatenate(
            [lax.dynamic_slice_in_dim(grad_pre_one, i * share, share, 1) for i in (index, index ^ 1)], axis=1
        )

    sent = [share_of((pts_index + 2 * by) % pts_count) for by in range(chips)]
    readout_rows = grad_readout.astype(jnp.bfloat16).reshape(-1, 2 * share)
    readout_rows = jnp.pad(readout_rows, ((0, 16 - readout_rows.shape[0]), (0, 0)))
    mine = jnp.concatenate([sent[0]] + [shift(sent[by], by) for by in range(1, chips)] + [readout_rows], axis=0)
    draws = redraws(1, [mine])
    _, mark = next(draws)
    if rows_local == LANES:
        cotangent = [mine] + [along(mine, by) for by in range(1, outer)] + [across(mine)]
        got, mark = stack(mark, *cotangent[1:outer])
        got = across(got)
        cotangent += [got[i] for i in range(outer - 1)]
        places = [(other, shift) for other in range(2) for shift in range(outer)]
        turn = base
    else:
        gathered = lax.all_gather(mine, "coord", axis=0)
        cotangent = [gathered[i] for i in range(coord_count)]
        turn = jnp.zeros_like(base)
    def add(kept, *received):
        return sum((a.astype(jnp.float32) for a in received), kept.astype(jnp.float32)).astype(jnp.bfloat16)

    def pick(a, index, axis):
        return lax.dynamic_index_in_dim(a, index, axis, keepdims=False)

    def rotate(a, by):
        return lax.ppermute(a, "pts", [(i, (i + by) % pts_count) for i in range(pts_count)])

    chip, core = pts_index // 2, pts_index % 2
    place, parity = coord_index // 2, coord_index % 2
    swap = [(i, i ^ 1) for i in range(pts_count)]
    quarter = hidden // coord_count // pts_count
    second = lax.dot_general(
        grad_pre_two, hidden_one, (((0,), (0,)), ((), ())), preferred_element_type=jnp.float32
    ).astype(jnp.bfloat16).reshape(coord_count, chips, 2, quarter, hidden)
    second = add(pick(second, core, 2), lax.ppermute(pick(second, 1 - core, 2), "pts", swap))
    drawn_second, last_mark = draws.send([mark, second])
    drawn = [drawn_first, drawn_second]
    second = add(
        pick(second, chip, 1), *[shift(pick(second, (chip + by) % chips, 1), by) for by in range(1, chips)]
    ).reshape(outer, 2, quarter, hidden)
    marks = [[second, last_mark]]
    second = add(pick(second, parity, 1), across(pick(second, 1 - parity, 1)))

    summed = sum(part.astype(jnp.float32) for part in cotangent)
    bias_half = jnp.sum(summed[:chips * rows_local], axis=0)
    readout = summed[chips * rows_local:chips * rows_local + pts_count // 2].reshape(-1)
    bias = jnp.zeros((hidden,), jnp.float32)
    for number, index in enumerate((pts_index, pts_index ^ 1)):
        bias = lax.dynamic_update_slice_in_dim(bias, bias_half[number * share:(number + 1) * share], index * share, 0)
    vectors = jnp.stack([bias, readout]).reshape(-1, LANES)
    vectors = vectors + sum(rotate(vectors, by) for by in range(1, pts_count))
    marks.append([second, vectors])
    second = add(
        pick(second, place, 0), *[along(pick(second, (place + by) % outer, 0), by) for by in range(1, outer)]
    )
    marks.append([second])
    blocks = jnp.zeros((pts_count, quarter, hidden), jnp.float32)
    for by in range(pts_count):
        block = rotate(second, by) if by else second
        blocks = lax.dynamic_update_index_in_dim(blocks, block.astype(jnp.float32), (pts_index - by) % pts_count, 0)
    second = blocks.reshape(pts_count * quarter, hidden)
    bias, readout = (
        lax.dynamic_slice_in_dim(v, coord_index * (hidden // coord_count), hidden // coord_count, 0)
        for v in vectors.reshape(2, hidden)
    )

    if rows_local != LANES:
        rows = jnp.stack(cotangent)[:, :chips * rows_local].reshape(coord_count, chips, rows_local, -1)
        rows = rows.transpose(1, 0, 2, 3).reshape(chips, -1, LANES, 2 * share).transpose(1, 0, 2, 3)
        rows = rows.reshape(-1, chips * LANES, 2 * share)
        cotangent = [rows[i] for i in range(rows.shape[0])]
        places = [(i % 2, -(i // 2) % (len(cotangent) // 2)) for i in range(len(cotangent))]

    def part(after, number, first, count, joined=None):
        keep, send, *out = gradient(
            turn, after, cotangent, places, own, drawn[number], width, first, count, cuts[number][0], valid, joined
        )
        return keep, lax.ppermute(send, "pts", swap), *out

    late = 2 if cuts[1][1] % 2 == 0 else 1
    middle = cuts[1][1] - late
    one = part(marks[0], 0, *cuts[0])
    two = part(marks[1], 1, early, middle)
    *three, out = part(marks[2], 1, early + middle, late, one)
    for (keep, got), first, size in ((two, early, middle), (three, early + middle, late)):
        wide = width * math.gcd(size, first, 2)
        out = join([], keep, got, out, wide, first * width // wide, valid)
    return (residual, out.T, second, bias, readout)


def solution(mesh):
    return jax.shard_map(
        shards,
        mesh=mesh,
        in_specs=(P("pts"), P("pts", None), P("coord"), P(None, "coord"), P(), P(), P()),
        out_specs=(
            P(("pts", "coord")),
            P("pts", "coord"),
            P("coord", None),
            P("coord"),
            P("coord"),
        ),
        check_vma=False,
    )
```

```python
import functools
import math

import jax
import jax.numpy as jnp
import numpy as np
from jax import lax
from jax.experimental import pallas as pl
from jax.experimental.pallas import tpu as pltpu
from jax.sharding import PartitionSpec as P

D = 100000

HASH_FACTOR = 73244475
NOISE_SCALE = 2.0
READOUT = 0.0625
LANES = 128
GROUP = 256
MASK = 8388607
VMEM_BYTES = 56 * 1024 * 1024

C0, C1, C2, C3 = 6.283164044286755, -2.583571398038591, 0.3177373780982648, -0.017332380925367475
B0, B1, B2 = C0 / C3, C1 / C3, C2 / C3
SINE_SCALE = -C3 * 2.0**-23
LOG_SCALE = -2.0 * (NOISE_SCALE * SINE_SCALE) ** 2


def shuffle_bits(bits):
    return bits ^ lax.shift_right_logical(bits, jnp.full_like(bits, 16))


def mix_tail(bits):
    bits = shuffle_bits(bits * HASH_FACTOR)
    return shuffle_bits(bits * HASH_FACTOR)


def mix_bits(bits):
    return mix_tail(shuffle_bits(bits))


def turn_wave(index):
    y = 2097152.0 - jnp.abs(index.astype(jnp.float32) + (0.5 - 4194304.0))
    s = (y * y) * 2.0**-42
    m = ((s + B2) * s + B1) * s + B0
    return y, m


def spread_seeds(seeds_ref, point_ref, pert, point):
    samples, points = seeds_ref.shape
    seeds = shuffle_bits(seeds_ref[...])
    for number in range(points):
        pert[number * samples:(number + 1) * samples] = jnp.broadcast_to(seeds[:, number:number + 1], (samples, LANES))
    point[...] = jnp.broadcast_to(shuffle_bits(point_ref[...]), (LANES, points)).T


def tile_lanes(a, width):
    return jnp.concatenate([a] * (width // a.shape[1]), axis=1)


def column_keys(base, step, width):
    columns = lax.broadcasted_iota(jnp.int32, (8, width), 1) + step * width
    four = (columns + base) * 4
    return columns, [shuffle_bits(mix_bits(four + t)) for t in range(3)]


def draw(seeds, key_zero, key_one):
    width = key_zero.shape[1]
    seeds = tile_lanes(seeds, width)
    first = mix_tail(seeds ^ jnp.concatenate([key_zero] * 2, axis=0))
    second = mix_tail(seeds ^ jnp.concatenate([key_one] * 2, axis=0))
    u0 = ((first & MASK).astype(jnp.float32) + 0.5) * 2.0**-23
    n = jnp.log(u0) * LOG_SCALE
    y, m = turn_wave(second & MASK)
    return ((n * lax.rsqrt(n)) * y) * m


def pieces(width):
    tiles = width // LANES
    parts = -(-tiles // 2)
    edges = [tiles * i // parts for i in range(parts + 1)]
    return [(a * LANES, b * LANES) for a, b in zip(edges, edges[1:])]


def point_rows(seeds, key, width):
    return mix_tail(tile_lanes(seeds, width) ^ key) & MASK


def coordinate(index):
    return (index.astype(jnp.float32) + (0.5 - 4194304.0)) * 2.0**-22


def forward_kernel(
    valid, base_ref, seeds_ref, spots_ref, coef_ref, w_prev, w_now, z_ref, *refs,
):
    near_ref, far_ref, held_a, held_b, acc, keys, xs, sq_ref, src_ref, sums, pert_ref, point_ref = refs
    step, last = pl.program_id(0), pl.num_programs(0) - 1
    rows, width = z_ref.shape
    points = point_ref.shape[0]
    samples = rows // points
    groups = rows // GROUP
    steps = -(-valid // width)
    pad = steps * width - valid

    @pl.when(step == 0)
    def _():
        acc[...] = jnp.zeros_like(acc)
        held_b[...] = jnp.zeros_like(held_b)
        sq_ref[...] = jnp.zeros_like(sq_ref)
        src_ref[...] = jnp.zeros_like(src_ref)
        spread_seeds(seeds_ref, spots_ref, pert_ref, point_ref)

    columns, (key_zero, key_one, key_two) = column_keys(base_ref[0], step, width)
    keys[0:8] = key_zero
    keys[8:16] = key_one
    inside = columns < valid
    coef = jnp.where(inside, jnp.broadcast_to(coef_ref[...], (8, width)), 0.0)
    for at in range(0, points, 8):
        index = point_rows(point_ref[at:at + 8], key_two, width)
        xs[at:at + 8] = coordinate(index)
        y, m = turn_wave((index + 2097152) & MASK)
        term = ((y * SINE_SCALE) * m) * coef
        src_ref[at:at + 8] += sum(
            term[:, a:a + LANES] for a in range(0, width, LANES)
        )

    cut = width - -(-pad // 16) * 16

    def multiply(group, part, held, ref, of):
        at, left = group * GROUP, part * GROUP
        w = ref[:, left:left + GROUP]
        if pad:
            place = lax.broadcasted_iota(jnp.int32, (width - cut, GROUP), 0) + (of * width + cut)
            tail = jnp.where(place < valid, w[cut:], jnp.zeros((), w.dtype))
            w = jnp.concatenate([w[:cut], tail], axis=0)
        acc[at:at + GROUP, left:left + GROUP] += jnp.dot(
            held[...], w, preferred_element_type=jnp.float32
        )

    parts = acc.shape[1] // GROUP
    group_points = GROUP // samples

    for group in range(groups):
        held = (held_a, held_b)[group % 2]
        other = (held_b, held_a)[group % 2]
        for number in range(group_points):
            if number % (group_points // parts) == 0:
                part = number // (group_points // parts)
                if group == 0:
                    multiply(groups - 1, part, other, w_prev, jnp.maximum(step - 1, 0))
                else:
                    multiply(group - 1, part, other, w_now, step)
            at = number * samples
            row = group * GROUP + at
            point = row // samples
            seeds = pert_ref[row:row + samples]
            total = None
            for a, b in pieces(width):
                noise = draw(seeds, keys[0:8, a:b], keys[8:16, a:b])
                x = jnp.broadcast_to(xs[point:point + 1, a:b], (samples, b - a))
                z = (x + noise).astype(jnp.bfloat16)
                held[at:at + samples, a:b] = z
                z_ref[row:row + samples, a:b] = z
                square = noise * noise
                for c in range(a, b, LANES):
                    cell = square[:, c - a:c - a + LANES]
                    if (steps - 1) * width + c + LANES > valid:
                        cell = jnp.where(jnp.concatenate([inside[:, c:c + LANES]] * 2, axis=0), cell, 0.0)
                    total = cell if total is None else total + cell
            sq_ref[row:row + samples] += total

    @pl.when(step == last)
    def _():
        for part in range(parts):
            multiply(groups - 1, part, held_b, w_now, step)
        sums[...] = jnp.zeros_like(sums)
        source = jnp.sum(src_ref[...].T, axis=0, keepdims=True) / math.sqrt(D)
        for block in range(rows // LANES):
            square = jnp.sum(sq_ref[block * LANES:(block + 1) * LANES].T, axis=0, keepdims=True)
            for at, left in ((0, square / NOISE_SCALE**2), (LANES, source)):
                sums[block * 16:block * 16 + 3, at:at + left.shape[1]] = three_terms(left)
        per = near_ref.shape[1] - 16
        outer = near_ref.shape[0]
        for other, ref in enumerate((near_ref, far_ref)):
            for shift in range(outer):
                to = lax.rem(lax.div(base_ref[1], 2) + shift, outer) * 2 + (base_ref[1] + other) % 2
                ref[shift, :per] = acc[pl.ds(pl.multiple_of(to * per, per), per), :].astype(ref.dtype)
                ref[shift, per:] = jnp.zeros((16, ref.shape[2]), ref.dtype)
                block = lax.div(to * per, LANES)
                ref[shift, per:, :2 * LANES] = sums[pl.ds(pl.multiple_of(block * 16, 16), 16), :].astype(ref.dtype)


def three_terms(left):
    terms = []
    for _ in range(3):
        terms.append(left.astype(jnp.bfloat16).astype(jnp.float32))
        left = left - terms[-1]
    return jnp.concatenate(terms, axis=0)


def combine_kernel(near_ref, got_ref, _, *out_refs):
    per = near_ref.shape[1] - 16
    for shift, ref in enumerate(out_refs):
        both = near_ref[shift].astype(jnp.float32) + got_ref[shift].astype(jnp.float32)
        ref[:per] = both[:per].astype(ref.dtype)
        terms = three_terms(jnp.sum(both[per:per + 3, :2 * LANES], axis=0, keepdims=True))
        ref[per:] = jnp.zeros((16, ref.shape[1]), ref.dtype)
        ref[per:, :2 * LANES] = jnp.concatenate([terms, jnp.zeros((13, 2 * LANES), jnp.float32)], axis=0).astype(ref.dtype)


def stack_kernel(_, *refs):
    *in_refs, out_ref, mark_ref = refs
    mark_ref[...] = jnp.zeros_like(mark_ref)
    for number, ref in enumerate(in_refs):
        out_ref[number] = ref[...]


def redraw_kernel(first, base_ref, seeds_ref, spots_ref, *refs):
    z_ref, mark_ref, keys, xs, pert_ref, point_ref = refs[-6:]

    @pl.when(pl.program_id(0) == 0)
    def _():
        spread_seeds(seeds_ref, spots_ref, pert_ref, point_ref)

    step = pl.program_id(0) + first
    rows, width = z_ref.shape
    points = point_ref.shape[0]
    samples = rows // points
    _, (key_zero, key_one, key_two) = column_keys(base_ref[0], step, width)
    keys[0:8] = key_zero
    keys[8:16] = key_one
    mark_ref[...] = jnp.zeros_like(mark_ref)
    for at in range(0, points, 8):
        xs[at:at + 8] = coordinate(point_rows(point_ref[at:at + 8], key_two, width))

    @pl.loop(0, points // 8)
    def _(block):
        eight = xs[pl.ds(pl.multiple_of(block * 8, 8), 8)]
        for inner in range(8):
            row = pl.multiple_of((block * 8 + inner) * samples, samples)
            seeds = pert_ref[pl.ds(row, samples)]
            for a, b in pieces(width):
                noise = draw(seeds, keys[0:8, a:b], keys[8:16, a:b])
                x = jnp.broadcast_to(eight[inner:inner + 1, a:b], (samples, b - a))
                z_ref[pl.ds(row, samples), a:b] = (x + noise).astype(jnp.bfloat16)


def gradient_kernel(count, places, skip, joins, base_ref, *refs):
    refs = refs[skip:]
    if joins:
        keep, got, *refs, out_ref, mark_ref, left = refs
        out_ref[...] = (keep[...].astype(jnp.float32) + got[...].astype(jnp.float32)).astype(jnp.bfloat16)
        refs = [*refs, mark_ref, left]
    d_refs, refs = refs[:len(places)], refs[len(places):]
    blocks = len(places)
    z_refs, (keep_ref, send_ref, mark_ref, left) = refs[:count], refs[count:]
    mark_ref[...] = jnp.zeros_like(mark_ref)
    half = keep_ref.shape[1]

    @pl.when(pl.program_id(0) == 0)
    def _():
        outer = blocks // 2
        for (other, shift), ref in zip(places, d_refs):
            block = lax.rem(lax.div(base_ref[1], 2) + outer - shift, outer) * 2 + (base_ref[1] + other) % 2
            for source in range(count):
                at = pl.multiple_of((source * blocks + block) * LANES, LANES)
                left[:, pl.ds(at, LANES)] = ref[source * LANES:(source + 1) * LANES, :].T

    width = keep_ref.shape[0]
    for a in range(0, width, 1024):
        b = min(a + 1024, width)
        z = jnp.concatenate([ref[:, a:b] for ref in z_refs], axis=0)
        part = jnp.dot(left[...], z, preferred_element_type=jnp.float32).astype(jnp.bfloat16).T
        keep_ref[a:b, :] = part[:, :half]
        send_ref[a:b, :] = part[:, half:]


def join_kernel(*refs):
    keep_ref, got_ref, out_ref = refs[0], refs[1], refs[-1]
    out_ref[...] = (keep_ref[...].astype(jnp.float32) + got_ref[...].astype(jnp.float32)).astype(jnp.bfloat16)


def params():
    return pltpu.CompilerParams(dimension_semantics=("arbitrary",), vmem_limit_bytes=VMEM_BYTES)


def whole(shape):
    return pl.BlockSpec(shape, lambda s: (0,) * len(shape))


def forward(base, pert, point, coef, w, width, parts):
    valid, hidden = w.shape
    rows, points = pert.size, point.size
    steps = -(-valid // width)
    smem = pl.BlockSpec(memory_space=pltpu.SMEM)
    return pl.pallas_call(
        functools.partial(forward_kernel, valid),
        grid=(steps,),
        in_specs=[
            smem, whole(pert.shape), whole(point.shape),
            pl.BlockSpec((1, width), lambda s: (0, s)),
            pl.BlockSpec((width, hidden), lambda s: (jnp.maximum(s - 1, 0), 0)),
            pl.BlockSpec((width, hidden), lambda s: (s, 0)),
        ],
        out_specs=[
            pl.BlockSpec((rows, width), lambda s: (0, s)),
        ] + [whole((parts // 2, rows // parts + 16, hidden))] * 2,
        out_shape=[
            jax.ShapeDtypeStruct((rows, steps * width), jnp.bfloat16),
        ] + [jax.ShapeDtypeStruct((parts // 2, rows // parts + 16, hidden), jnp.bfloat16)] * 2,
        scratch_shapes=[
            pltpu.VMEM((GROUP, width), jnp.bfloat16),
            pltpu.VMEM((GROUP, width), jnp.bfloat16),
            pltpu.VMEM((rows, hidden), jnp.float32),
            pltpu.VMEM((16, width), jnp.int32),
            pltpu.VMEM((points, width), jnp.float32),
            pltpu.VMEM((rows, LANES), jnp.float32),
            pltpu.VMEM((points, LANES), jnp.float32),
            pltpu.VMEM((rows // LANES * 16, 2 * LANES), jnp.float32),
            pltpu.VMEM((rows, LANES), jnp.int32),
            pltpu.VMEM((points, LANES), jnp.int32),
        ],
        compiler_params=params(),
        cost_estimate=pl.CostEstimate(
            flops=100 * rows * valid * 40, bytes_accessed=4 * rows * valid, transcendentals=2 * rows * valid
        ),
        name="forward",
    )(base, pert, point, coef, w, w)


def redraw(base, pert, point, after, before, width, first, count, start, total):
    rows, points = pert.size, point.size
    anywhere = pl.BlockSpec(memory_space=pl.ANY)
    extra = [] if before is None else [before]
    return pl.pallas_call(
        functools.partial(redraw_kernel, first),
        grid=(count,),
        in_specs=[pl.BlockSpec(memory_space=pltpu.SMEM), whole(pert.shape), whole(point.shape)]
        + [anywhere] * (len(after) + len(extra)),
        out_specs=[pl.BlockSpec((rows, width), lambda s: (0, s + first - start)), whole((8, LANES))],
        out_shape=[
            jax.ShapeDtypeStruct((rows, total * width), jnp.bfloat16),
            jax.ShapeDtypeStruct((8, LANES), jnp.float32),
        ],
        input_output_aliases={3 + len(after): 0} if extra else {},
        scratch_shapes=[
            pltpu.VMEM((16, width), jnp.int32), pltpu.VMEM((points, width), jnp.float32),
            pltpu.VMEM((rows, LANES), jnp.int32), pltpu.VMEM((points, LANES), jnp.int32),
        ],
        compiler_params=params(),
        cost_estimate=pl.CostEstimate(
            flops=100 * rows * width * count * 40, bytes_accessed=2 * rows * width * count, transcendentals=0,
        ),
        name="redraw",
    )(base, pert, point, *after, *extra)


def combine(near, got, after):
    parts, rows, hidden = near.shape
    return pl.pallas_call(
        combine_kernel,
        grid=(1,),
        in_specs=[whole(near.shape)] * 2 + [pl.BlockSpec(memory_space=pl.ANY)],
        out_specs=[whole((rows, hidden))] * parts,
        out_shape=[jax.ShapeDtypeStruct((rows, hidden), jnp.bfloat16)] * parts,
        compiler_params=params(),
        cost_estimate=pl.CostEstimate(flops=parts * rows * hidden, bytes_accessed=6 * parts * rows * hidden, transcendentals=0),
        name="combine",
    )(near, got, after)


def stack(after, *arrays):
    shape = arrays[0].shape
    return pl.pallas_call(
        stack_kernel,
        grid=(1,),
        in_specs=[pl.BlockSpec(memory_space=pl.ANY)] + [whole(shape)] * len(arrays),
        out_specs=[whole((len(arrays), *shape)), whole((8, LANES))],
        out_shape=[
            jax.ShapeDtypeStruct((len(arrays), *shape), arrays[0].dtype),
            jax.ShapeDtypeStruct((8, LANES), jnp.float32),
        ],
        compiler_params=params(),
        cost_estimate=pl.CostEstimate(flops=0, bytes_accessed=4 * len(arrays) * math.prod(shape), transcendentals=0),
        name="stack",
    )(after, *arrays)


def gradient(base, after, cotangent, places, own, others, width, first, count, start, valid, joined=None):
    if joined is None and all(n % 2 == 0 for n in (count, first, start)):
        width, first, count, start = 2 * width, first // 2, count // 2, start // 2
    rows = own.shape[0]
    half = cotangent[0].shape[1] // 2
    height = min(valid, (first + count) * width) - first * width
    out_specs = [pl.BlockSpec((width, half), lambda s: (s, 0))] * 2
    out_shape = [jax.ShapeDtypeStruct((height, half), jnp.bfloat16)] * 2
    joins, spec = [], None
    if joined is not None:
        joins = list(joined)
        spec = pl.BlockSpec((joins[0].shape[0] // count, half), lambda s: (s, 0))
        out_specs, out_shape = out_specs + [spec], out_shape + [jax.ShapeDtypeStruct((valid, half), jnp.bfloat16)]
    out_specs, out_shape = out_specs + [whole((8, LANES))], out_shape + [jax.ShapeDtypeStruct((8, LANES), jnp.float32)]
    return pl.pallas_call(
        functools.partial(gradient_kernel, 1 + len(others), places, len(after), len(joins) > 0),
        grid=(count,),
        in_specs=[pl.BlockSpec(memory_space=pltpu.SMEM)] + [pl.BlockSpec(memory_space=pl.ANY)] * len(after)
        + [spec] * len(joins)
        + [whole(part.shape) for part in cotangent]
        + [pl.BlockSpec((rows, width), lambda s: (0, s + first))]
        + [pl.BlockSpec((rows, width), lambda s: (0, s + first - start)) for _ in others],
        out_specs=out_specs,
        out_shape=out_shape,
        scratch_shapes=[pltpu.VMEM((2 * half, (1 + len(others)) * rows), jnp.bfloat16)],
        compiler_params=params(),
        cost_estimate=pl.CostEstimate(
            flops=100 * rows * width * count * 40, bytes_accessed=2 * rows * width * count, transcendentals=0,
        ),
        name="gradient",
    )(base, *after, *joins, *cotangent, own, *others)


def join(after, keep, got, before, width, first, valid):
    height, half = keep.shape
    count = -(-height // width)
    anywhere = pl.BlockSpec(memory_space=pl.ANY)
    specs = [pl.BlockSpec((width, half), lambda s: (s, 0))] * 2 + [anywhere] * len(after)
    operands, aliases = [keep, got, *after], {}
    if before is not None:
        specs, operands, aliases = specs + [anywhere], operands + [before], {len(operands): 0}
    return pl.pallas_call(
        join_kernel,
        grid=(count,),
        in_specs=specs,
        out_specs=pl.BlockSpec((width, half), lambda s: (s + first, 0)),
        out_shape=jax.ShapeDtypeStruct((valid, half), jnp.bfloat16),
        input_output_aliases=aliases,
        compiler_params=params(),
        cost_estimate=pl.CostEstimate(flops=height * half, bytes_accessed=6 * height * half, transcendentals=0),
        name="join",
    )(*operands)


def hidden_kernel(samples, count, chips, base_ref, _, *refs):
    part_refs, (b1_ref, w2_ref, w3_ref), refs = refs[:count], refs[count:count + 3], refs[count + 3:]
    residual_ref, kept_ref, sent_ref, *share_refs, first, second = refs
    rows = part_refs[0].shape[0] - 16
    coord, pts = base_ref[1], base_ref[2]
    total = sum(ref[...].astype(jnp.float32) for ref in part_refs)
    sums = jnp.sum(total[rows:rows + 3, :2 * LANES], axis=0, keepdims=True)
    row = lax.broadcasted_iota(jnp.int32, (rows, LANES), 0)
    lane = lax.broadcasted_iota(jnp.int32, (rows, LANES), 1)

    def choose(values, index):
        return jnp.sum(jnp.where(lane == index, values, 0.0), axis=1, keepdims=True)

    point = lax.div(row, samples)
    squares = choose(sums[:, :LANES], row + lax.rem(coord * rows, LANES))
    source = choose(sums[:, LANES:], point + coord * (rows // samples))
    one = jnp.tanh(total[:rows] + b1_ref[...]).astype(jnp.bfloat16)
    two = jnp.tanh(
        lax.dot_general(one, w2_ref[...], (((1,), (1,)), ((), ())), preferred_element_type=jnp.float32)
    ).astype(jnp.bfloat16).astype(jnp.float32)
    w3 = w3_ref[...]
    values = READOUT * jnp.sum(two * w3, axis=1, keepdims=True)
    stein = (squares - D) / (NOISE_SCALE * NOISE_SCALE * samples)
    terms = jnp.broadcast_to(stein * values, (rows, LANES))
    if rows < LANES:
        terms = jnp.concatenate([terms, jnp.zeros((LANES - rows, LANES), jnp.float32)], axis=0)
    terms = jnp.where(lax.div(lane, samples) == point, terms.T[:rows], 0.0)
    residual = jnp.sum(terms, axis=1, keepdims=True) - source
    for number in range(rows // samples):
        residual_ref[number:number + 1] = jnp.broadcast_to(residual[number * samples:number * samples + 1], (1, LANES))
    cotangent = residual * stein
    readout = READOUT * jnp.sum(cotangent * two, axis=0, keepdims=True)
    pre_two = (READOUT * cotangent * w3 * (1.0 - two * two)).astype(jnp.bfloat16)
    wide = one.astype(jnp.float32)
    pre_one = jnp.dot(pre_two, w2_ref[...], preferred_element_type=jnp.float32) * (1.0 - wide * wide)
    first[...] = pre_one.astype(jnp.bfloat16)
    bias = jnp.sum(first[...].astype(jnp.float32), axis=0, keepdims=True)
    share = first.shape[1] // (2 * chips)
    for by, ref in enumerate(share_refs):
        chip = lax.rem(lax.div(pts, 2) + by, chips)
        for half in range(2):
            index = chip * 2 + (pts + half) % 2
            ref[:, half * share:(half + 1) * share] = first[:, pl.ds(pl.multiple_of(index * share, share), share)]
    height, wide = kept_ref.shape[3] - 16, first.shape[1]
    outer = kept_ref.shape[2]
    second[:wide] = jnp.dot(pre_two.T, one, preferred_element_type=jnp.float32).astype(jnp.bfloat16)
    second[wide:] = jnp.concatenate([readout, bias, jnp.zeros((14, wide), jnp.float32)], axis=0).astype(jnp.bfloat16)
    for other_core, ref in enumerate((kept_ref, sent_ref)):
        for by in range(chips):
            index = lax.rem(lax.div(pts, 2) + by, chips) * 2 + (pts + other_core) % 2
            lanes = pl.ds(pl.multiple_of(index * share, share), share)
            for other in range(2):
                for shift in range(outer):
                    block = lax.rem(lax.div(coord, 2) + shift, outer) * 2 + (coord + other) % 2
                    rows_of = pl.ds(pl.multiple_of(block * height, height), height)
                    ref[by, other, shift, :height] = second[rows_of, lanes]
                    ref[by, other, shift, height:] = second[wide:, lanes]


def hidden_layers(base, after, parts, b1, w2, w3, samples, chips, blocks):
    rows, hidden = parts[0].shape[0] - 16, parts[0].shape[1]
    shapes = [(rows // samples, LANES)] + [(chips, 2, blocks // 2, hidden // blocks + 16, hidden // chips // 2)] * 2
    shapes += [(rows, hidden // chips)] * chips
    types = [jnp.float32] + [jnp.bfloat16] * (2 + chips)
    operands = [*parts, b1[None, :], w2, w3.astype(jnp.float32)[None, :]]
    return pl.pallas_call(
        functools.partial(hidden_kernel, samples, len(parts), chips),
        grid=(1,),
        in_specs=[pl.BlockSpec(memory_space=pltpu.SMEM), pl.BlockSpec(memory_space=pl.ANY)]
        + [whole(a.shape) for a in operands],
        out_specs=[whole(shape) for shape in shapes],
        out_shape=[jax.ShapeDtypeStruct(shape, kind) for shape, kind in zip(shapes, types)],
        scratch_shapes=[pltpu.VMEM((rows, hidden), jnp.bfloat16), pltpu.VMEM((hidden + 16, hidden), jnp.bfloat16)],
        compiler_params=params(),
        cost_estimate=pl.CostEstimate(
            flops=6 * rows * hidden * hidden, bytes_accessed=4 * hidden * hidden, transcendentals=2 * rows * hidden
        ),
        name="hidden",
    )(base, after, *operands)


def block_width(valid):
    tiles = -(-valid // LANES)
    best = min((8, 7, 6, 5), key=lambda t: -(-tiles // t) * t)
    return best * LANES


def shards(point_seed, pert_seed, source_coef, w1, b1, w2, w3):
    coord_count = lax.axis_size("coord")
    pts_count = lax.axis_size("pts")
    chips = pts_count // 2
    hidden, valid = w1.shape
    points_here, samples = pert_seed.shape
    rows_here = points_here * samples
    rows_local = rows_here // coord_count
    points_local = points_here // coord_count
    coord_index = lax.axis_index("coord")
    pts_index = lax.axis_index("pts")
    share = hidden // pts_count
    width = block_width(valid)
    steps = -(-valid // width)
    base = jnp.stack([coord_index * valid, coord_index, pts_index]).astype(jnp.int32)

    def shift(a, by):
        return jax.tree.map(
            lambda leaf: lax.ppermute(
                leaf, "pts", [(i, (i + 2 * by) % pts_count) for i in range(pts_count)]
            ), a,
        )

    other_seeds = [shift((pert_seed, point_seed), by) for by in range(1, chips)]

    pert, point = pert_seed.T, point_seed[None, :]
    own, near, far = forward(base, pert, point, source_coef[None, :], w1.T, width, coord_count)
    others_in = [(a.T, b[None, :]) for a, b in other_seeds]
    outer = coord_count // 2

    def across(a):
        return lax.ppermute(a, "coord", [(i, i ^ 1) for i in range(coord_count)])

    def along(a, by):
        return lax.ppermute(a, "coord", [(i, (i + 2 * by) % coord_count) for i in range(coord_count)])

    early = steps // 2 + (steps // 2) % 2
    cuts = [(0, early), (early, steps - early)]

    def redraws(number, after):
        first, count = cuts[number]
        held = [None] * len(others_in)
        for at, size in ((0, -(-count // 2)), (-(-count // 2), count // 2)):
            made = [
                redraw(base, a, b, after, z, width, first + at, size, first, count)
                for (a, b), z in zip(others_in, held)
            ]
            held = [z for z, _ in made]
            after = yield held, sum(mark for _, mark in made)

    draws = redraws(0, [near])
    _, mark = next(draws)
    parts = combine(near, across(far), mark)
    drawn_first, mark = draws.send([parts[0]])
    parts = [parts[0]] + [along(parts[by], by) for by in range(1, outer)]
    residual, kept, given, *sent = hidden_layers(base, mark, parts, b1, w2, w3, samples, chips, coord_count)
    residual = residual[:, 0]
    mine = jnp.concatenate([sent[0]] + [shift(sent[by], by) for by in range(1, chips)], axis=0)
    draws = redraws(1, [mine])
    _, mark = next(draws)
    if rows_local == LANES:
        cotangent = [mine] + [along(mine, by) for by in range(1, outer)] + [across(mine)]
        got, mark = stack(mark, *cotangent[1:outer])
        got = across(got)
        cotangent += [got[i] for i in range(outer - 1)]
        places = [(other, shift) for other in range(2) for shift in range(outer)]
        turn = base
    else:
        gathered = lax.all_gather(mine, "coord", axis=0)
        cotangent = [gathered[i] for i in range(coord_count)]
        turn = jnp.zeros_like(base)
    def add(own_part, *received):
        return sum((a.astype(jnp.float32) for a in received), own_part.astype(jnp.float32)).astype(jnp.bfloat16)

    swap = [(i, i ^ 1) for i in range(pts_count)]
    second = add(kept, lax.ppermute(given, "pts", swap))
    drawn_second, last_mark = draws.send([mark, second])
    drawn = [drawn_first, drawn_second]
    second = add(second[0], *[shift(second[by], by) for by in range(1, chips)])
    if rows_local != LANES:
        rows = jnp.stack(cotangent)[:, :chips * rows_local].reshape(coord_count, chips, rows_local, -1)
        rows = rows.transpose(1, 0, 2, 3).reshape(chips, -1, LANES, 2 * share).transpose(1, 0, 2, 3)
        rows = rows.reshape(-1, chips * LANES, 2 * share)
        cotangent = [rows[i] for i in range(rows.shape[0])]
        places = [(i % 2, -(i // 2) % (len(cotangent) // 2)) for i in range(len(cotangent))]

    def part(after, number, first, count, joined=None):
        keep, send, *out, mark = gradient(
            turn, after, cotangent, places, own, drawn[number], width, first, count, cuts[number][0], valid, joined
        )
        return mark[0, 0], keep, lax.ppermute(send, "pts", swap), *out

    late = 2 if cuts[1][1] % 2 == 0 else 1
    middle = cuts[1][1] - late
    mark, *one = part([second, last_mark], 0, *cuts[0])
    second = add(second[0], across(second[1]), mark)
    mark, *two = part([second], 1, early, middle)
    second = add(second[0], *[along(second[by], by) for by in range(1, outer)], mark)
    _, *three, out = part([second], 1, early + middle, late, one)
    height = hidden // coord_count
    joined = jnp.zeros((second.shape[0], hidden), jnp.float32)
    for by in range(pts_count):
        block = second if by == 0 else lax.ppermute(second, "pts", [(i, (i + by) % pts_count) for i in range(pts_count)])
        joined = lax.dynamic_update_slice_in_dim(
            joined, block.astype(jnp.float32), (pts_index - by) % pts_count * share, 1
        )
    readout, bias = (
        lax.dynamic_slice_in_dim(joined[row], coord_index * height, height, 0) for row in (height, height + 1)
    )
    second = joined[:height]

    for (keep, got), first, size in ((two, early, middle), (three, early + middle, late)):
        wide = width * math.gcd(size, first, 2)
        out = join([], keep, got, out, wide, first * width // wide, valid)
    return (residual, out.T, second, bias, readout)


def solution(mesh):
    return jax.shard_map(
        shards,
        mesh=mesh,
        in_specs=(P("pts"), P("pts", None), P("coord"), P(None, "coord"), P(), P(), P()),
        out_specs=(
            P(("pts", "coord")),
            P("pts", "coord"),
            P("coord", None),
            P("coord"),
            P("coord"),
        ),
        check_vma=False,
    )
```

```python
import functools
import math

import jax
import jax.numpy as jnp
import numpy as np
from jax import lax
from jax.experimental import pallas as pl
from jax.experimental.pallas import tpu as pltpu
from jax.sharding import PartitionSpec as P

D = 100000

HASH_FACTOR = 73244475
NOISE_SCALE = 2.0
READOUT = 0.0625
LANES = 128
GROUP = 256
MASK = 8388607
VMEM_BYTES = 56 * 1024 * 1024

C0, C1, C2, C3 = 6.283164044286755, -2.583571398038591, 0.3177373780982648, -0.017332380925367475
B0, B1, B2 = C0 / C3, C1 / C3, C2 / C3
SINE_SCALE = -C3 * 2.0**-23
LOG_SCALE = -2.0 * (NOISE_SCALE * SINE_SCALE) ** 2


def shuffle_bits(bits):
    return bits ^ lax.shift_right_logical(bits, jnp.full_like(bits, 16))


def mix_tail(bits):
    bits = shuffle_bits(bits * HASH_FACTOR)
    return shuffle_bits(bits * HASH_FACTOR)


def mix_bits(bits):
    return mix_tail(shuffle_bits(bits))


def turn_wave(index):
    y = 2097152.0 - jnp.abs(index.astype(jnp.float32) + (0.5 - 4194304.0))
    s = (y * y) * 2.0**-42
    m = ((s + B2) * s + B1) * s + B0
    return y, m


def spread_seeds(seeds_ref, point_ref, pert, point):
    samples, points = seeds_ref.shape
    seeds = shuffle_bits(seeds_ref[...])
    for number in range(points):
        pert[number * samples:(number + 1) * samples] = jnp.broadcast_to(seeds[:, number:number + 1], (samples, LANES))
    point[...] = jnp.broadcast_to(shuffle_bits(point_ref[...]), (LANES, points)).T


def tile_lanes(a, width):
    return jnp.concatenate([a] * (width // a.shape[1]), axis=1)


def column_keys(base, step, width):
    columns = lax.broadcasted_iota(jnp.int32, (8, width), 1) + step * width
    four = (columns + base) * 4
    return columns, [shuffle_bits(mix_bits(four + t)) for t in range(3)]


def draw(seeds, key_zero, key_one):
    width = key_zero.shape[1]
    seeds = tile_lanes(seeds, width)
    first = mix_tail(seeds ^ jnp.concatenate([key_zero] * 2, axis=0))
    second = mix_tail(seeds ^ jnp.concatenate([key_one] * 2, axis=0))
    u0 = ((first & MASK).astype(jnp.float32) + 0.5) * 2.0**-23
    n = jnp.log(u0) * LOG_SCALE
    y, m = turn_wave(second & MASK)
    return ((n * lax.rsqrt(n)) * y) * m


def pieces(width):
    tiles = width // LANES
    parts = -(-tiles // 2)
    edges = [tiles * i // parts for i in range(parts + 1)]
    return [(a * LANES, b * LANES) for a, b in zip(edges, edges[1:])]


def point_rows(seeds, key, width):
    return mix_tail(tile_lanes(seeds, width) ^ key) & MASK


def coordinate(index):
    return (index.astype(jnp.float32) + (0.5 - 4194304.0)) * 2.0**-22


def forward_kernel(
    valid, base_ref, seeds_ref, spots_ref, coef_ref, w_prev, w_now, z_ref, *refs,
):
    near_ref, far_ref, held_a, held_b, acc, keys, xs, sq_ref, src_ref, sums, pert_ref, point_ref = refs
    step, last = pl.program_id(0), pl.num_programs(0) - 1
    rows, width = z_ref.shape
    points = point_ref.shape[0]
    samples = rows // points
    half = width // 2
    steps = -(-valid // width)
    pad = steps * width - valid

    @pl.when(step == 0)
    def _():
        acc[...] = jnp.zeros_like(acc)
        held_b[...] = jnp.zeros_like(held_b)
        sq_ref[...] = jnp.zeros_like(sq_ref)
        src_ref[...] = jnp.zeros_like(src_ref)
        spread_seeds(seeds_ref, spots_ref, pert_ref, point_ref)

    columns, (key_zero, key_one, key_two) = column_keys(base_ref[0], step, width)
    keys[0:8] = key_zero
    keys[8:16] = key_one
    inside = columns < valid
    coef = jnp.where(inside, jnp.broadcast_to(coef_ref[...], (8, width)), 0.0)
    for at in range(0, points, 8):
        index = point_rows(point_ref[at:at + 8], key_two, width)
        xs[at:at + 8] = coordinate(index)
        y, m = turn_wave((index + 2097152) & MASK)
        term = ((y * SINE_SCALE) * m) * coef
        src_ref[at:at + 8] += sum(
            term[:, a:a + LANES] for a in range(0, width, LANES)
        )

    def multiply(at, left, held, w):
        block, lanes = slice(at, at + GROUP), pl.ds(left, GROUP)
        acc[block, lanes] += jnp.dot(held[block, :], w, preferred_element_type=jnp.float32)

    def phase(offset, held, other, w_ref, w_at):
        @pl.loop(0, rows // GROUP)
        def _(part):
            left = pl.multiple_of(part * GROUP, GROUP)
            w = w_ref[w_at:w_at + half, pl.ds(left, GROUP)]
            count = GROUP // samples
            for number in range(count):
                if number % (count // (rows // GROUP)) == 0:
                    multiply(number // (count // (rows // GROUP)) * GROUP, left, other, w)
                if number % 8 == 0:
                    eight = xs[pl.ds(pl.multiple_of(part * count + number, 8), 8), offset:offset + half]
                row = pl.multiple_of((part * count + number) * samples, samples)
                seeds = pert_ref[pl.ds(row, samples)]
                total = None
                for a, b in pieces(half):
                    noise = draw(seeds, keys[0:8, offset + a:offset + b], keys[8:16, offset + a:offset + b])
                    x = jnp.broadcast_to(eight[number % 8:number % 8 + 1, a:b], (samples, b - a))
                    z = (x + noise).astype(jnp.bfloat16)
                    held[pl.ds(row, samples), a:b] = z
                    z_ref[pl.ds(row, samples), offset + a:offset + b] = z
                    square = noise * noise
                    for c in range(a, b, LANES):
                        cell = square[:, c - a:c - a + LANES]
                        place = offset + c
                        if (steps - 1) * width + place + LANES > valid:
                            cell = jnp.where(
                                jnp.concatenate([inside[:, place:place + LANES]] * 2, axis=0), cell, 0.0
                            )
                        total = cell if total is None else total + cell
                sq_ref[pl.ds(row, samples)] += total

    phase(0, held_a, held_b, w_prev, 0)
    phase(half, held_b, held_a, w_now, 0)

    @pl.when(step == last)
    def _():
        place = lax.broadcasted_iota(jnp.int32, (half, GROUP), 0)
        for left in range(0, acc.shape[1], GROUP):
            w = w_now[half:, left:left + GROUP]
            w = jnp.where(place < half - pad, w, jnp.zeros((), w.dtype))
            for at in range(0, rows, GROUP):
                multiply(at, left, held_b, w)
        sums[...] = jnp.zeros_like(sums)
        source = jnp.sum(src_ref[...].T, axis=0, keepdims=True) / math.sqrt(D)
        for block in range(rows // LANES):
            square = jnp.sum(sq_ref[block * LANES:(block + 1) * LANES].T, axis=0, keepdims=True)
            for at, left in ((0, square / NOISE_SCALE**2), (LANES, source)):
                sums[block * 16:block * 16 + 3, at:at + left.shape[1]] = three_terms(left)
        per = near_ref.shape[1] - 16
        outer = near_ref.shape[0]
        for other, ref in enumerate((near_ref, far_ref)):
            for shift in range(outer):
                to = lax.rem(lax.div(base_ref[1], 2) + shift, outer) * 2 + (base_ref[1] + other) % 2
                ref[shift, :per] = acc[pl.ds(pl.multiple_of(to * per, per), per), :].astype(ref.dtype)
                ref[shift, per:] = jnp.zeros((16, ref.shape[2]), ref.dtype)
                block = lax.div(to * per, LANES)
                ref[shift, per:, :2 * LANES] = sums[pl.ds(pl.multiple_of(block * 16, 16), 16), :].astype(ref.dtype)


def three_terms(left):
    terms = []
    for _ in range(3):
        terms.append(left.astype(jnp.bfloat16).astype(jnp.float32))
        left = left - terms[-1]
    return jnp.concatenate(terms, axis=0)


def combine_kernel(near_ref, got_ref, _, *out_refs):
    per = near_ref.shape[1] - 16
    for shift, ref in enumerate(out_refs):
        both = near_ref[shift].astype(jnp.float32) + got_ref[shift].astype(jnp.float32)
        ref[:per] = both[:per].astype(ref.dtype)
        terms = three_terms(jnp.sum(both[per:per + 3, :2 * LANES], axis=0, keepdims=True))
        ref[per:] = jnp.zeros((16, ref.shape[1]), ref.dtype)
        ref[per:, :2 * LANES] = jnp.concatenate([terms, jnp.zeros((13, 2 * LANES), jnp.float32)], axis=0).astype(ref.dtype)


def stack_kernel(_, *refs):
    *in_refs, out_ref, mark_ref = refs
    mark_ref[...] = jnp.zeros_like(mark_ref)
    for number, ref in enumerate(in_refs):
        out_ref[number] = ref[...]


def redraw_kernel(first, base_ref, seeds_ref, spots_ref, *refs):
    z_ref, mark_ref, keys, xs, pert_ref, point_ref = refs[-6:]

    @pl.when(pl.program_id(0) == 0)
    def _():
        spread_seeds(seeds_ref, spots_ref, pert_ref, point_ref)

    step = pl.program_id(0) + first
    rows, width = z_ref.shape
    points = point_ref.shape[0]
    samples = rows // points
    _, (key_zero, key_one, key_two) = column_keys(base_ref[0], step, width)
    keys[0:8] = key_zero
    keys[8:16] = key_one
    mark_ref[...] = jnp.zeros_like(mark_ref)
    for at in range(0, points, 8):
        xs[at:at + 8] = coordinate(point_rows(point_ref[at:at + 8], key_two, width))

    @pl.loop(0, points // 8)
    def _(block):
        eight = xs[pl.ds(pl.multiple_of(block * 8, 8), 8)]
        for inner in range(8):
            row = pl.multiple_of((block * 8 + inner) * samples, samples)
            seeds = pert_ref[pl.ds(row, samples)]
            for a, b in pieces(width):
                noise = draw(seeds, keys[0:8, a:b], keys[8:16, a:b])
                x = jnp.broadcast_to(eight[inner:inner + 1, a:b], (samples, b - a))
                z_ref[pl.ds(row, samples), a:b] = (x + noise).astype(jnp.bfloat16)


def gradient_kernel(count, places, skip, joins, base_ref, *refs):
    refs = refs[skip:]
    if joins:
        keep, got, *refs, out_ref, mark_ref, left = refs
        out_ref[...] = (keep[...].astype(jnp.float32) + got[...].astype(jnp.float32)).astype(jnp.bfloat16)
        refs = [*refs, mark_ref, left]
    d_refs, refs = refs[:len(places)], refs[len(places):]
    blocks = len(places)
    z_refs, (keep_ref, send_ref, mark_ref, left) = refs[:count], refs[count:]
    mark_ref[...] = jnp.zeros_like(mark_ref)
    half = keep_ref.shape[1]

    @pl.when(pl.program_id(0) == 0)
    def _():
        outer = blocks // 2
        for (other, shift), ref in zip(places, d_refs):
            block = lax.rem(lax.div(base_ref[1], 2) + outer - shift, outer) * 2 + (base_ref[1] + other) % 2
            for source in range(count):
                at = pl.multiple_of((source * blocks + block) * LANES, LANES)
                left[:, pl.ds(at, LANES)] = ref[source * LANES:(source + 1) * LANES, :].T

    width = keep_ref.shape[0]
    for a in range(0, width, 1024):
        b = min(a + 1024, width)
        z = jnp.concatenate([ref[:, a:b] for ref in z_refs], axis=0)
        part = jnp.dot(left[...], z, preferred_element_type=jnp.float32).astype(jnp.bfloat16).T
        keep_ref[a:b, :] = part[:, :half]
        send_ref[a:b, :] = part[:, half:]


def join_kernel(*refs):
    keep_ref, got_ref, out_ref, mark_ref = refs[0], refs[1], refs[-2], refs[-1]
    mark_ref[...] = jnp.zeros_like(mark_ref)
    out_ref[...] = (keep_ref[...].astype(jnp.float32) + got_ref[...].astype(jnp.float32)).astype(jnp.bfloat16)


def params():
    return pltpu.CompilerParams(dimension_semantics=("arbitrary",), vmem_limit_bytes=VMEM_BYTES)


def whole(shape):
    return pl.BlockSpec(shape, lambda s: (0,) * len(shape))


def forward(base, pert, point, coef, w, width, parts):
    valid, hidden = w.shape
    rows, points = pert.size, point.size
    steps = -(-valid // width)
    smem = pl.BlockSpec(memory_space=pltpu.SMEM)
    return pl.pallas_call(
        functools.partial(forward_kernel, valid),
        grid=(steps,),
        in_specs=[
            smem, whole(pert.shape), whole(point.shape),
            pl.BlockSpec((1, width), lambda s: (0, s)),
            pl.BlockSpec((width // 2, hidden), lambda s: (jnp.maximum(2 * s - 1, 0), 0)),
            pl.BlockSpec((width, hidden), lambda s: (s, 0)),
        ],
        out_specs=[
            pl.BlockSpec((rows, width), lambda s: (0, s)),
        ] + [whole((parts // 2, rows // parts + 16, hidden))] * 2,
        out_shape=[
            jax.ShapeDtypeStruct((rows, steps * width), jnp.bfloat16),
        ] + [jax.ShapeDtypeStruct((parts // 2, rows // parts + 16, hidden), jnp.bfloat16)] * 2,
        scratch_shapes=[
            pltpu.VMEM((rows, width // 2), jnp.bfloat16),
            pltpu.VMEM((rows, width // 2), jnp.bfloat16),
            pltpu.VMEM((rows, hidden), jnp.float32),
            pltpu.VMEM((16, width), jnp.int32),
            pltpu.VMEM((points, width), jnp.float32),
            pltpu.VMEM((rows, LANES), jnp.float32),
            pltpu.VMEM((points, LANES), jnp.float32),
            pltpu.VMEM((rows // LANES * 16, 2 * LANES), jnp.float32),
            pltpu.VMEM((rows, LANES), jnp.int32),
            pltpu.VMEM((points, LANES), jnp.int32),
        ],
        compiler_params=params(),
        cost_estimate=pl.CostEstimate(
            flops=100 * rows * valid * 40, bytes_accessed=4 * rows * valid, transcendentals=2 * rows * valid
        ),
        name="forward",
    )(base, pert, point, coef, w, w)


def redraw(base, pert, point, after, before, width, first, count, start, total):
    rows, points = pert.size, point.size
    anywhere = pl.BlockSpec(memory_space=pl.ANY)
    extra = [] if before is None else [before]
    return pl.pallas_call(
        functools.partial(redraw_kernel, first),
        grid=(count,),
        in_specs=[pl.BlockSpec(memory_space=pltpu.SMEM), whole(pert.shape), whole(point.shape)]
        + [anywhere] * (len(after) + len(extra)),
        out_specs=[pl.BlockSpec((rows, width), lambda s: (0, s + first - start)), whole((8, LANES))],
        out_shape=[
            jax.ShapeDtypeStruct((rows, total * width), jnp.bfloat16),
            jax.ShapeDtypeStruct((8, LANES), jnp.float32),
        ],
        input_output_aliases={3 + len(after): 0} if extra else {},
        scratch_shapes=[
            pltpu.VMEM((16, width), jnp.int32), pltpu.VMEM((points, width), jnp.float32),
            pltpu.VMEM((rows, LANES), jnp.int32), pltpu.VMEM((points, LANES), jnp.int32),
        ],
        compiler_params=params(),
        cost_estimate=pl.CostEstimate(
            flops=100 * rows * width * count * 40, bytes_accessed=2 * rows * width * count, transcendentals=0,
        ),
        name="redraw",
    )(base, pert, point, *after, *extra)


def combine(near, got, after):
    parts, rows, hidden = near.shape
    return pl.pallas_call(
        combine_kernel,
        grid=(1,),
        in_specs=[whole(near.shape)] * 2 + [pl.BlockSpec(memory_space=pl.ANY)],
        out_specs=[whole((rows, hidden))] * parts,
        out_shape=[jax.ShapeDtypeStruct((rows, hidden), jnp.bfloat16)] * parts,
        compiler_params=params(),
        cost_estimate=pl.CostEstimate(flops=parts * rows * hidden, bytes_accessed=6 * parts * rows * hidden, transcendentals=0),
        name="combine",
    )(near, got, after)


def stack(after, *arrays):
    shape = arrays[0].shape
    return pl.pallas_call(
        stack_kernel,
        grid=(1,),
        in_specs=[pl.BlockSpec(memory_space=pl.ANY)] + [whole(shape)] * len(arrays),
        out_specs=[whole((len(arrays), *shape)), whole((8, LANES))],
        out_shape=[
            jax.ShapeDtypeStruct((len(arrays), *shape), arrays[0].dtype),
            jax.ShapeDtypeStruct((8, LANES), jnp.float32),
        ],
        compiler_params=params(),
        cost_estimate=pl.CostEstimate(flops=0, bytes_accessed=4 * len(arrays) * math.prod(shape), transcendentals=0),
        name="stack",
    )(after, *arrays)


def gradient(base, after, cotangent, places, own, others, width, first, count, start, valid, joined=None):
    if joined is None and all(n % 2 == 0 for n in (count, first, start)):
        width, first, count, start = 2 * width, first // 2, count // 2, start // 2
    rows = own.shape[0]
    half = cotangent[0].shape[1] // 2
    height = min(valid, (first + count) * width) - first * width
    out_specs = [pl.BlockSpec((width, half), lambda s: (s, 0))] * 2
    out_shape = [jax.ShapeDtypeStruct((height, half), jnp.bfloat16)] * 2
    joins, spec = [], None
    if joined is not None:
        joins = list(joined)
        spec = pl.BlockSpec((joins[0].shape[0] // count, half), lambda s: (s, 0))
        out_specs, out_shape = out_specs + [spec], out_shape + [jax.ShapeDtypeStruct((valid, half), jnp.bfloat16)]
    out_specs, out_shape = out_specs + [whole((8, LANES))], out_shape + [jax.ShapeDtypeStruct((8, LANES), jnp.float32)]
    return pl.pallas_call(
        functools.partial(gradient_kernel, 1 + len(others), places, len(after), len(joins) > 0),
        grid=(count,),
        in_specs=[pl.BlockSpec(memory_space=pltpu.SMEM)] + [pl.BlockSpec(memory_space=pl.ANY)] * len(after)
        + [spec] * len(joins)
        + [whole(part.shape) for part in cotangent]
        + [pl.BlockSpec((rows, width), lambda s: (0, s + first))]
        + [pl.BlockSpec((rows, width), lambda s: (0, s + first - start)) for _ in others],
        out_specs=out_specs,
        out_shape=out_shape,
        scratch_shapes=[pltpu.VMEM((2 * half, (1 + len(others)) * rows), jnp.bfloat16)],
        compiler_params=params(),
        cost_estimate=pl.CostEstimate(
            flops=100 * rows * width * count * 40, bytes_accessed=2 * rows * width * count, transcendentals=0,
        ),
        name="gradient",
    )(base, *after, *joins, *cotangent, own, *others)


def join(after, keep, got, before, width, first, valid):
    height, half = keep.shape
    count = -(-height // width)
    anywhere = pl.BlockSpec(memory_space=pl.ANY)
    specs = [pl.BlockSpec((width, half), lambda s: (s, 0))] * 2 + [anywhere] * len(after)
    operands, aliases = [keep, got, *after], {}
    if before is not None:
        specs, operands, aliases = specs + [anywhere], operands + [before], {len(operands): 0}
    return pl.pallas_call(
        join_kernel,
        grid=(count,),
        in_specs=specs,
        out_specs=[pl.BlockSpec((width, half), lambda s: (s + first, 0)), whole((8, LANES))],
        out_shape=[
            jax.ShapeDtypeStruct((valid, half), jnp.bfloat16), jax.ShapeDtypeStruct((8, LANES), jnp.float32),
        ],
        input_output_aliases=aliases,
        compiler_params=params(),
        cost_estimate=pl.CostEstimate(
            flops=100 * height * half * 100, bytes_accessed=6 * height * half, transcendentals=0
        ),
        name="join",
    )(*operands)


def hidden_kernel(samples, count, chips, base_ref, _, *refs):
    part_refs, (b1_ref, w2_ref, w3_ref), refs = refs[:count], refs[count:count + 3], refs[count + 3:]
    residual_ref, kept_ref, sent_ref, *share_refs, first, second = refs
    rows = part_refs[0].shape[0] - 16
    coord, pts = base_ref[1], base_ref[2]
    total = sum(ref[...].astype(jnp.float32) for ref in part_refs)
    sums = jnp.sum(total[rows:rows + 3, :2 * LANES], axis=0, keepdims=True)
    row = lax.broadcasted_iota(jnp.int32, (rows, LANES), 0)
    lane = lax.broadcasted_iota(jnp.int32, (rows, LANES), 1)

    def choose(values, index):
        return jnp.sum(jnp.where(lane == index, values, 0.0), axis=1, keepdims=True)

    point = lax.div(row, samples)
    squares = choose(sums[:, :LANES], row + lax.rem(coord * rows, LANES))
    source = choose(sums[:, LANES:], point + coord * (rows // samples))
    one = jnp.tanh(total[:rows] + b1_ref[...]).astype(jnp.bfloat16)
    two = jnp.tanh(
        lax.dot_general(one, w2_ref[...], (((1,), (1,)), ((), ())), preferred_element_type=jnp.float32)
    ).astype(jnp.bfloat16).astype(jnp.float32)
    w3 = w3_ref[...]
    values = READOUT * jnp.sum(two * w3, axis=1, keepdims=True)
    stein = (squares - D) / (NOISE_SCALE * NOISE_SCALE * samples)
    terms = jnp.broadcast_to(stein * values, (rows, LANES))
    if rows < LANES:
        terms = jnp.concatenate([terms, jnp.zeros((LANES - rows, LANES), jnp.float32)], axis=0)
    terms = jnp.where(lax.div(lane, samples) == point, terms.T[:rows], 0.0)
    residual = jnp.sum(terms, axis=1, keepdims=True) - source
    for number in range(rows // samples):
        residual_ref[number:number + 1] = jnp.broadcast_to(residual[number * samples:number * samples + 1], (1, LANES))
    cotangent = residual * stein
    readout = READOUT * jnp.sum(cotangent * two, axis=0, keepdims=True)
    pre_two = (READOUT * cotangent * w3 * (1.0 - two * two)).astype(jnp.bfloat16)
    wide = one.astype(jnp.float32)
    pre_one = jnp.dot(pre_two, w2_ref[...], preferred_element_type=jnp.float32) * (1.0 - wide * wide)
    first[...] = pre_one.astype(jnp.bfloat16)
    bias = jnp.sum(first[...].astype(jnp.float32), axis=0, keepdims=True)
    share = first.shape[1] // (2 * chips)
    for by, ref in enumerate(share_refs):
        chip = lax.rem(lax.div(pts, 2) + by, chips)
        for half in range(2):
            index = chip * 2 + (pts + half) % 2
            ref[:, half * share:(half + 1) * share] = first[:, pl.ds(pl.multiple_of(index * share, share), share)]
    height, wide = kept_ref.shape[3] - 16, first.shape[1]
    outer = kept_ref.shape[2]
    second[:wide] = jnp.dot(pre_two.T, one, preferred_element_type=jnp.float32).astype(jnp.bfloat16)
    second[wide:] = jnp.concatenate([readout, bias, jnp.zeros((14, wide), jnp.float32)], axis=0).astype(jnp.bfloat16)
    for other_core, ref in enumerate((kept_ref, sent_ref)):
        for by in range(chips):
            index = lax.rem(lax.div(pts, 2) + by, chips) * 2 + (pts + other_core) % 2
            lanes = pl.ds(pl.multiple_of(index * share, share), share)
            for other in range(2):
                for shift in range(outer):
                    block = lax.rem(lax.div(coord, 2) + shift, outer) * 2 + (coord + other) % 2
                    rows_of = pl.ds(pl.multiple_of(block * height, height), height)
                    ref[by, other, shift, :height] = second[rows_of, lanes]
                    ref[by, other, shift, height:] = second[wide:, lanes]


def hidden_layers(base, after, parts, b1, w2, w3, samples, chips, blocks):
    rows, hidden = parts[0].shape[0] - 16, parts[0].shape[1]
    shapes = [(rows // samples, LANES)] + [(chips, 2, blocks // 2, hidden // blocks + 16, hidden // chips // 2)] * 2
    shapes += [(rows, hidden // chips)] * chips
    types = [jnp.float32] + [jnp.bfloat16] * (2 + chips)
    operands = [*parts, b1[None, :], w2, w3.astype(jnp.float32)[None, :]]
    return pl.pallas_call(
        functools.partial(hidden_kernel, samples, len(parts), chips),
        grid=(1,),
        in_specs=[pl.BlockSpec(memory_space=pltpu.SMEM), pl.BlockSpec(memory_space=pl.ANY)]
        + [whole(a.shape) for a in operands],
        out_specs=[whole(shape) for shape in shapes],
        out_shape=[jax.ShapeDtypeStruct(shape, kind) for shape, kind in zip(shapes, types)],
        scratch_shapes=[pltpu.VMEM((rows, hidden), jnp.bfloat16), pltpu.VMEM((hidden + 16, hidden), jnp.bfloat16)],
        compiler_params=params(),
        cost_estimate=pl.CostEstimate(
            flops=6 * rows * hidden * hidden, bytes_accessed=4 * hidden * hidden, transcendentals=2 * rows * hidden
        ),
        name="hidden",
    )(base, after, *operands)


def block_width(valid):
    tiles = -(-valid // LANES)
    best = min((8, 7, 6, 5), key=lambda t: (-(-tiles // t) % 2, -(-tiles // t) * t))
    return best * LANES


def shards(point_seed, pert_seed, source_coef, w1, b1, w2, w3):
    coord_count = lax.axis_size("coord")
    pts_count = lax.axis_size("pts")
    chips = pts_count // 2
    hidden, valid = w1.shape
    points_here, samples = pert_seed.shape
    rows_here = points_here * samples
    rows_local = rows_here // coord_count
    points_local = points_here // coord_count
    coord_index = lax.axis_index("coord")
    pts_index = lax.axis_index("pts")
    share = hidden // pts_count
    width = block_width(valid)
    steps = -(-valid // width)
    base = jnp.stack([coord_index * valid, coord_index, pts_index]).astype(jnp.int32)

    def shift(a, by):
        return jax.tree.map(
            lambda leaf: lax.ppermute(
                leaf, "pts", [(i, (i + 2 * by) % pts_count) for i in range(pts_count)]
            ), a,
        )

    other_seeds = [shift((pert_seed, point_seed), by) for by in range(1, chips)]

    pert, point = pert_seed.T, point_seed[None, :]
    own, near, far = forward(base, pert, point, source_coef[None, :], w1.T, 2 * width, coord_count)
    others_in = [(a.T, b[None, :]) for a, b in other_seeds]
    outer = coord_count // 2

    def across(a):
        return lax.ppermute(a, "coord", [(i, i ^ 1) for i in range(coord_count)])

    def along(a, by):
        return lax.ppermute(a, "coord", [(i, (i + 2 * by) % coord_count) for i in range(coord_count)])

    early = steps // 2 + (steps // 2) % 2
    cuts = [(0, early), (early, steps - early)]

    def redraws(number, after):
        first, count = cuts[number]
        held = [None] * len(others_in)
        for at, size in ((0, -(-count // 2)), (-(-count // 2), count // 2)):
            made = [
                redraw(base, a, b, after, z, width, first + at, size, first, count)
                for (a, b), z in zip(others_in, held)
            ]
            held = [z for z, _ in made]
            after = yield held, sum(mark for _, mark in made)

    draws = redraws(0, [near])
    _, mark = next(draws)
    parts = combine(near, across(far), mark)
    drawn_first, mark = draws.send([parts[0]])
    parts = [parts[0]] + [along(parts[by], by) for by in range(1, outer)]
    residual, kept, given, *sent = hidden_layers(base, mark, parts, b1, w2, w3, samples, chips, coord_count)
    residual = residual[:, 0]
    mine = jnp.concatenate([sent[0]] + [shift(sent[by], by) for by in range(1, chips)], axis=0)
    draws = redraws(1, [mine])
    _, mark = next(draws)
    if rows_local == LANES:
        cotangent = [mine] + [along(mine, by) for by in range(1, outer)] + [across(mine)]
        got, mark = stack(mark, *cotangent[1:outer])
        got = across(got)
        cotangent += [got[i] for i in range(outer - 1)]
        places = [(other, shift) for other in range(2) for shift in range(outer)]
        turn = base
    else:
        gathered = lax.all_gather(mine, "coord", axis=0)
        cotangent = [gathered[i] for i in range(coord_count)]
        turn = jnp.zeros_like(base)
    def add(own_part, *received):
        return sum((a.astype(jnp.float32) for a in received), own_part.astype(jnp.float32)).astype(jnp.bfloat16)

    swap = [(i, i ^ 1) for i in range(pts_count)]
    second = add(kept, lax.ppermute(given, "pts", swap))
    drawn_second, last_mark = draws.send([mark, second])
    drawn = [drawn_first, drawn_second]
    second = add(second[0], *[shift(second[by], by) for by in range(1, chips)])
    if rows_local != LANES:
        rows = jnp.stack(cotangent)[:, :chips * rows_local].reshape(coord_count, chips, rows_local, -1)
        rows = rows.transpose(1, 0, 2, 3).reshape(chips, -1, LANES, 2 * share).transpose(1, 0, 2, 3)
        rows = rows.reshape(-1, chips * LANES, 2 * share)
        cotangent = [rows[i] for i in range(rows.shape[0])]
        places = [(i % 2, -(i // 2) % (len(cotangent) // 2)) for i in range(len(cotangent))]

    def part(after, number, first, count, joined=None):
        keep, send, *out, mark = gradient(
            turn, after, cotangent, places, own, drawn[number], width, first, count, cuts[number][0], valid, joined
        )
        return mark[0, 0], keep, lax.ppermute(send, "pts", swap), *out

    mark, *one = part([second, last_mark], 0, *cuts[0])
    second = add(second[0], across(second[1]), mark)
    _, *two = part([second], 1, *cuts[1])

    def place(after, part, cut, out):
        (keep, got), (first, size) = part, cut
        wide = width * math.gcd(size, first, 2)
        out, mark = join(after, keep, got, out, wide, first * width // wide, valid)
        return out, mark[0, 0]

    out, mark = place([], one, cuts[0], None)
    second = add(second[0], *[along(second[by], by) for by in range(1, outer)], mark)
    out, mark = place([second], two, cuts[1], out)
    height = hidden // coord_count
    joined = jnp.zeros((second.shape[0], hidden), jnp.float32) + mark
    for by in range(pts_count):
        block = second if by == 0 else lax.ppermute(second, "pts", [(i, (i + by) % pts_count) for i in range(pts_count)])
        joined = lax.dynamic_update_slice_in_dim(
            joined, block.astype(jnp.float32), (pts_index - by) % pts_count * share, 1
        )
    readout, bias = (
        lax.dynamic_slice_in_dim(joined[row], coord_index * height, height, 0) for row in (height, height + 1)
    )
    second = joined[:height]

    return (residual, out.T, second, bias, readout)


def solution(mesh):
    return jax.shard_map(
        shards,
        mesh=mesh,
        in_specs=(P("pts"), P("pts", None), P("coord"), P(None, "coord"), P(), P(), P()),
        out_specs=(
            P(("pts", "coord")),
            P("pts", "coord"),
            P("coord", None),
            P("coord"),
            P("coord"),
        ),
        check_vma=False,
    )
```

```python
import functools
import math

import jax
import jax.numpy as jnp
import numpy as np
from jax import lax
from jax.experimental import pallas as pl
from jax.experimental.pallas import tpu as pltpu
from jax.sharding import PartitionSpec as P

D = 100000

HASH_FACTOR = 73244475
NOISE_SCALE = 2.0
READOUT = 0.0625
LANES = 128
GROUP = 256
MASK = 8388607
VMEM_BYTES = 56 * 1024 * 1024

C0, C1, C2, C3 = 6.283164044286755, -2.583571398038591, 0.3177373780982648, -0.017332380925367475
B0, B1, B2 = C0 / C3, C1 / C3, C2 / C3
SINE_SCALE = -C3 * 2.0**-23
LOG_SCALE = -2.0 * (NOISE_SCALE * SINE_SCALE) ** 2


def shuffle_bits(bits):
    return bits ^ lax.shift_right_logical(bits, jnp.full_like(bits, 16))


def mix_tail(bits):
    bits = shuffle_bits(bits * HASH_FACTOR)
    return shuffle_bits(bits * HASH_FACTOR)


def mix_bits(bits):
    return mix_tail(shuffle_bits(bits))


def turn_wave(index):
    y = 2097152.0 - jnp.abs(index.astype(jnp.float32) + (0.5 - 4194304.0))
    s = (y * y) * 2.0**-42
    m = ((s + B2) * s + B1) * s + B0
    return y, m


def spread_seeds(seeds_ref, point_ref, pert, point):
    samples, points = seeds_ref.shape
    seeds = shuffle_bits(seeds_ref[...])
    for number in range(points):
        pert[number * samples:(number + 1) * samples] = jnp.broadcast_to(seeds[:, number:number + 1], (samples, LANES))
    point[...] = jnp.broadcast_to(shuffle_bits(point_ref[...]), (LANES, points)).T


def tile_lanes(a, width):
    return jnp.concatenate([a] * (width // a.shape[1]), axis=1)


def column_keys(base, step, width):
    columns = lax.broadcasted_iota(jnp.int32, (8, width), 1) + step * width
    four = (columns + base) * 4
    return columns, [shuffle_bits(mix_bits(four + t)) for t in range(3)]


def draw(seeds, key_zero, key_one):
    width = key_zero.shape[1]
    seeds = tile_lanes(seeds, width)
    first = mix_tail(seeds ^ jnp.concatenate([key_zero] * 2, axis=0))
    second = mix_tail(seeds ^ jnp.concatenate([key_one] * 2, axis=0))
    u0 = ((first & MASK).astype(jnp.float32) + 0.5) * 2.0**-23
    n = jnp.log(u0) * LOG_SCALE
    y, m = turn_wave(second & MASK)
    return ((n * lax.rsqrt(n)) * y) * m


def pieces(width):
    tiles = width // LANES
    parts = -(-tiles // 2)
    edges = [tiles * i // parts for i in range(parts + 1)]
    return [(a * LANES, b * LANES) for a, b in zip(edges, edges[1:])]


def point_rows(seeds, key, width):
    return mix_tail(tile_lanes(seeds, width) ^ key) & MASK


def coordinate(index):
    return (index.astype(jnp.float32) + (0.5 - 4194304.0)) * 2.0**-22


def forward_kernel(
    valid, base_ref, seeds_ref, spots_ref, coef_ref, w_prev, w_now, z_ref, *refs,
):
    near_ref, far_ref, held_a, held_b, acc, keys, xs, sq_ref, src_ref, sums, pert_ref, point_ref = refs
    step, last = pl.program_id(0), pl.num_programs(0) - 1
    rows, width = z_ref.shape
    points = point_ref.shape[0]
    samples = rows // points
    groups = rows // GROUP
    steps = -(-valid // width)
    pad = steps * width - valid

    @pl.when(step == 0)
    def _():
        acc[...] = jnp.zeros_like(acc)
        held_b[...] = jnp.zeros_like(held_b)
        sq_ref[...] = jnp.zeros_like(sq_ref)
        src_ref[...] = jnp.zeros_like(src_ref)
        spread_seeds(seeds_ref, spots_ref, pert_ref, point_ref)

    columns, (key_zero, key_one, key_two) = column_keys(base_ref[0], step, width)
    keys[0:8] = key_zero
    keys[8:16] = key_one
    inside = columns < valid
    coef = jnp.where(inside, jnp.broadcast_to(coef_ref[...], (8, width)), 0.0)
    for at in range(0, points, 8):
        index = point_rows(point_ref[at:at + 8], key_two, width)
        xs[at:at + 8] = coordinate(index)
        y, m = turn_wave((index + 2097152) & MASK)
        term = ((y * SINE_SCALE) * m) * coef
        src_ref[at:at + 8] += sum(
            term[:, a:a + LANES] for a in range(0, width, LANES)
        )

    cut = width - -(-pad // 16) * 16

    def multiply(group, part, held, ref, of):
        at, left = group * GROUP, part * GROUP
        w = ref[:, left:left + GROUP]
        if pad:
            place = lax.broadcasted_iota(jnp.int32, (width - cut, GROUP), 0) + (of * width + cut)
            tail = jnp.where(place < valid, w[cut:], jnp.zeros((), w.dtype))
            w = jnp.concatenate([w[:cut], tail], axis=0)
        acc[at:at + GROUP, left:left + GROUP] += jnp.dot(
            held[...], w, preferred_element_type=jnp.float32
        )

    parts = acc.shape[1] // GROUP
    group_points = GROUP // samples

    for group in range(groups):
        held = (held_a, held_b)[group % 2]
        other = (held_b, held_a)[group % 2]
        for number in range(group_points):
            if number % (group_points // parts) == 0:
                part = number // (group_points // parts)
                if group == 0:
                    multiply(groups - 1, part, other, w_prev, jnp.maximum(step - 1, 0))
                else:
                    multiply(group - 1, part, other, w_now, step)
            at = number * samples
            row = group * GROUP + at
            point = row // samples
            seeds = pert_ref[row:row + samples]
            total = None
            for a, b in pieces(width):
                noise = draw(seeds, keys[0:8, a:b], keys[8:16, a:b])
                x = jnp.broadcast_to(xs[point:point + 1, a:b], (samples, b - a))
                z = (x + noise).astype(jnp.bfloat16)
                held[at:at + samples, a:b] = z
                z_ref[row:row + samples, a:b] = z
                square = noise * noise
                for c in range(a, b, LANES):
                    cell = square[:, c - a:c - a + LANES]
                    if (steps - 1) * width + c + LANES > valid:
                        cell = jnp.where(jnp.concatenate([inside[:, c:c + LANES]] * 2, axis=0), cell, 0.0)
                    total = cell if total is None else total + cell
            sq_ref[row:row + samples] += total

    @pl.when(step == last)
    def _():
        for part in range(parts):
            multiply(groups - 1, part, held_b, w_now, step)
        sums[...] = jnp.zeros_like(sums)
        source = jnp.sum(src_ref[...].T, axis=0, keepdims=True) / math.sqrt(D)
        for block in range(rows // LANES):
            square = jnp.sum(sq_ref[block * LANES:(block + 1) * LANES].T, axis=0, keepdims=True)
            for at, left in ((0, square / NOISE_SCALE**2), (LANES, source)):
                sums[block * 16:block * 16 + 3, at:at + left.shape[1]] = three_terms(left)
        per = near_ref.shape[1] - 16
        outer = near_ref.shape[0]
        for other, ref in enumerate((near_ref, far_ref)):
            for shift in range(outer):
                to = lax.rem(lax.div(base_ref[1], 2) + shift, outer) * 2 + (base_ref[1] + other) % 2
                ref[shift, :per] = acc[pl.ds(pl.multiple_of(to * per, per), per), :].astype(ref.dtype)
                ref[shift, per:] = jnp.zeros((16, ref.shape[2]), ref.dtype)
                block = lax.div(to * per, LANES)
                ref[shift, per:, :2 * LANES] = sums[pl.ds(pl.multiple_of(block * 16, 16), 16), :].astype(ref.dtype)


def three_terms(left):
    terms = []
    for _ in range(3):
        terms.append(left.astype(jnp.bfloat16).astype(jnp.float32))
        left = left - terms[-1]
    return jnp.concatenate(terms, axis=0)


def combine_kernel(near_ref, got_ref, _, *out_refs):
    per = near_ref.shape[1] - 16
    for shift, ref in enumerate(out_refs):
        both = near_ref[shift].astype(jnp.float32) + got_ref[shift].astype(jnp.float32)
        ref[:per] = both[:per].astype(ref.dtype)
        terms = three_terms(jnp.sum(both[per:per + 3, :2 * LANES], axis=0, keepdims=True))
        ref[per:] = jnp.zeros((16, ref.shape[1]), ref.dtype)
        ref[per:, :2 * LANES] = jnp.concatenate([terms, jnp.zeros((13, 2 * LANES), jnp.float32)], axis=0).astype(ref.dtype)


def stack_kernel(_, *refs):
    *in_refs, out_ref, mark_ref = refs
    mark_ref[...] = jnp.zeros_like(mark_ref)
    for number, ref in enumerate(in_refs):
        out_ref[number] = ref[...]


def redraw_kernel(first, base_ref, seeds_ref, spots_ref, *refs):
    z_ref, mark_ref, keys, xs, pert_ref, point_ref = refs[-6:]

    @pl.when(pl.program_id(0) == 0)
    def _():
        spread_seeds(seeds_ref, spots_ref, pert_ref, point_ref)

    step = pl.program_id(0) + first
    rows, width = z_ref.shape
    points = point_ref.shape[0]
    samples = rows // points
    _, (key_zero, key_one, key_two) = column_keys(base_ref[0], step, width)
    keys[0:8] = key_zero
    keys[8:16] = key_one
    mark_ref[...] = jnp.zeros_like(mark_ref)
    for at in range(0, points, 8):
        xs[at:at + 8] = coordinate(point_rows(point_ref[at:at + 8], key_two, width))

    @pl.loop(0, points // 8)
    def _(block):
        eight = xs[pl.ds(pl.multiple_of(block * 8, 8), 8)]
        for inner in range(8):
            row = pl.multiple_of((block * 8 + inner) * samples, samples)
            seeds = pert_ref[pl.ds(row, samples)]
            for a, b in pieces(width):
                noise = draw(seeds, keys[0:8, a:b], keys[8:16, a:b])
                x = jnp.broadcast_to(eight[inner:inner + 1, a:b], (samples, b - a))
                z_ref[pl.ds(row, samples), a:b] = (x + noise).astype(jnp.bfloat16)


def gradient_kernel(count, places, skip, joins, base_ref, *refs):
    refs = refs[skip:]
    if joins:
        keep, got, *refs, out_ref, mark_ref, left = refs
        out_ref[...] = (keep[...].astype(jnp.float32) + got[...].astype(jnp.float32)).astype(jnp.bfloat16)
        refs = [*refs, mark_ref, left]
    d_refs, refs = refs[:len(places)], refs[len(places):]
    blocks = len(places)
    z_refs, (keep_ref, send_ref, mark_ref, left) = refs[:count], refs[count:]
    mark_ref[...] = jnp.zeros_like(mark_ref)
    half = keep_ref.shape[1]

    @pl.when(pl.program_id(0) == 0)
    def _():
        outer = blocks // 2
        for (other, shift), ref in zip(places, d_refs):
            block = lax.rem(lax.div(base_ref[1], 2) + outer - shift, outer) * 2 + (base_ref[1] + other) % 2
            for source in range(count):
                at = pl.multiple_of((source * blocks + block) * LANES, LANES)
                left[:, pl.ds(at, LANES)] = ref[source * LANES:(source + 1) * LANES, :].T

    width = keep_ref.shape[0]
    for a in range(0, width, 1024):
        b = min(a + 1024, width)
        z = jnp.concatenate([ref[:, a:b] for ref in z_refs], axis=0)
        part = jnp.dot(left[...], z, preferred_element_type=jnp.float32).astype(jnp.bfloat16).T
        keep_ref[a:b, :] = part[:, :half]
        send_ref[a:b, :] = part[:, half:]


def join_kernel(*refs):
    keep_ref, got_ref, out_ref, mark_ref = refs[0], refs[1], refs[-2], refs[-1]
    mark_ref[...] = jnp.zeros_like(mark_ref)
    out_ref[...] = (keep_ref[...].astype(jnp.float32) + got_ref[...].astype(jnp.float32)).astype(jnp.bfloat16)


def params():
    return pltpu.CompilerParams(dimension_semantics=("arbitrary",), vmem_limit_bytes=VMEM_BYTES)


def whole(shape):
    return pl.BlockSpec(shape, lambda s: (0,) * len(shape))


def forward(base, pert, point, coef, w, width, parts):
    valid, hidden = w.shape
    rows, points = pert.size, point.size
    steps = -(-valid // width)
    smem = pl.BlockSpec(memory_space=pltpu.SMEM)
    return pl.pallas_call(
        functools.partial(forward_kernel, valid),
        grid=(steps,),
        in_specs=[
            smem, whole(pert.shape), whole(point.shape),
            pl.BlockSpec((1, width), lambda s: (0, s)),
            pl.BlockSpec((width, hidden), lambda s: (jnp.maximum(s - 1, 0), 0)),
            pl.BlockSpec((width, hidden), lambda s: (s, 0)),
        ],
        out_specs=[
            pl.BlockSpec((rows, width), lambda s: (0, s)),
        ] + [whole((parts // 2, rows // parts + 16, hidden))] * 2,
        out_shape=[
            jax.ShapeDtypeStruct((rows, steps * width), jnp.bfloat16),
        ] + [jax.ShapeDtypeStruct((parts // 2, rows // parts + 16, hidden), jnp.bfloat16)] * 2,
        scratch_shapes=[
            pltpu.VMEM((GROUP, width), jnp.bfloat16),
            pltpu.VMEM((GROUP, width), jnp.bfloat16),
            pltpu.VMEM((rows, hidden), jnp.float32),
            pltpu.VMEM((16, width), jnp.int32),
            pltpu.VMEM((points, width), jnp.float32),
            pltpu.VMEM((rows, LANES), jnp.float32),
            pltpu.VMEM((points, LANES), jnp.float32),
            pltpu.VMEM((rows // LANES * 16, 2 * LANES), jnp.float32),
            pltpu.VMEM((rows, LANES), jnp.int32),
            pltpu.VMEM((points, LANES), jnp.int32),
        ],
        compiler_params=params(),
        cost_estimate=pl.CostEstimate(
            flops=100 * rows * valid * 40, bytes_accessed=4 * rows * valid, transcendentals=2 * rows * valid
        ),
        name="forward",
    )(base, pert, point, coef, w, w)


def redraw(base, pert, point, after, before, width, first, count, start, total):
    rows, points = pert.size, point.size
    anywhere = pl.BlockSpec(memory_space=pl.ANY)
    extra = [] if before is None else [before]
    return pl.pallas_call(
        functools.partial(redraw_kernel, first),
        grid=(count,),
        in_specs=[pl.BlockSpec(memory_space=pltpu.SMEM), whole(pert.shape), whole(point.shape)]
        + [anywhere] * (len(after) + len(extra)),
        out_specs=[pl.BlockSpec((rows, width), lambda s: (0, s + first - start)), whole((8, LANES))],
        out_shape=[
            jax.ShapeDtypeStruct((rows, total * width), jnp.bfloat16),
            jax.ShapeDtypeStruct((8, LANES), jnp.float32),
        ],
        input_output_aliases={3 + len(after): 0} if extra else {},
        scratch_shapes=[
            pltpu.VMEM((16, width), jnp.int32), pltpu.VMEM((points, width), jnp.float32),
            pltpu.VMEM((rows, LANES), jnp.int32), pltpu.VMEM((points, LANES), jnp.int32),
        ],
        compiler_params=params(),
        cost_estimate=pl.CostEstimate(
            flops=100 * rows * width * count * 40, bytes_accessed=2 * rows * width * count, transcendentals=0,
        ),
        name="redraw",
    )(base, pert, point, *after, *extra)


def combine(near, got, after):
    parts, rows, hidden = near.shape
    return pl.pallas_call(
        combine_kernel,
        grid=(1,),
        in_specs=[whole(near.shape)] * 2 + [pl.BlockSpec(memory_space=pl.ANY)],
        out_specs=[whole((rows, hidden))] * parts,
        out_shape=[jax.ShapeDtypeStruct((rows, hidden), jnp.bfloat16)] * parts,
        compiler_params=params(),
        cost_estimate=pl.CostEstimate(flops=parts * rows * hidden, bytes_accessed=6 * parts * rows * hidden, transcendentals=0),
        name="combine",
    )(near, got, after)


def stack(after, *arrays):
    shape = arrays[0].shape
    return pl.pallas_call(
        stack_kernel,
        grid=(1,),
        in_specs=[pl.BlockSpec(memory_space=pl.ANY)] + [whole(shape)] * len(arrays),
        out_specs=[whole((len(arrays), *shape)), whole((8, LANES))],
        out_shape=[
            jax.ShapeDtypeStruct((len(arrays), *shape), arrays[0].dtype),
            jax.ShapeDtypeStruct((8, LANES), jnp.float32),
        ],
        compiler_params=params(),
        cost_estimate=pl.CostEstimate(flops=0, bytes_accessed=4 * len(arrays) * math.prod(shape), transcendentals=0),
        name="stack",
    )(after, *arrays)


def gradient(base, after, cotangent, places, own, others, width, first, count, start, valid, joined=None):
    if joined is None and all(n % 2 == 0 for n in (count, first, start)):
        width, first, count, start = 2 * width, first // 2, count // 2, start // 2
    rows = own.shape[0]
    half = cotangent[0].shape[1] // 2
    height = min(valid, (first + count) * width) - first * width
    out_specs = [pl.BlockSpec((width, half), lambda s: (s, 0))] * 2
    out_shape = [jax.ShapeDtypeStruct((height, half), jnp.bfloat16)] * 2
    joins, spec = [], None
    if joined is not None:
        joins = list(joined)
        spec = pl.BlockSpec((joins[0].shape[0] // count, half), lambda s: (s, 0))
        out_specs, out_shape = out_specs + [spec], out_shape + [jax.ShapeDtypeStruct((valid, half), jnp.bfloat16)]
    out_specs, out_shape = out_specs + [whole((8, LANES))], out_shape + [jax.ShapeDtypeStruct((8, LANES), jnp.float32)]
    return pl.pallas_call(
        functools.partial(gradient_kernel, 1 + len(others), places, len(after), len(joins) > 0),
        grid=(count,),
        in_specs=[pl.BlockSpec(memory_space=pltpu.SMEM)] + [pl.BlockSpec(memory_space=pl.ANY)] * len(after)
        + [spec] * len(joins)
        + [whole(part.shape) for part in cotangent]
        + [pl.BlockSpec((rows, width), lambda s: (0, s + first))]
        + [pl.BlockSpec((rows, width), lambda s: (0, s + first - start)) for _ in others],
        out_specs=out_specs,
        out_shape=out_shape,
        scratch_shapes=[pltpu.VMEM((2 * half, (1 + len(others)) * rows), jnp.bfloat16)],
        compiler_params=params(),
        cost_estimate=pl.CostEstimate(
            flops=100 * rows * width * count * 40, bytes_accessed=2 * rows * width * count, transcendentals=0,
        ),
        name="gradient",
    )(base, *after, *joins, *cotangent, own, *others)


def join(after, keep, got, before, width, first, valid):
    height, half = keep.shape
    count = -(-height // width)
    anywhere = pl.BlockSpec(memory_space=pl.ANY)
    specs = [pl.BlockSpec((width, half), lambda s: (s, 0))] * 2 + [anywhere] * len(after)
    operands, aliases = [keep, got, *after], {}
    if before is not None:
        specs, operands, aliases = specs + [anywhere], operands + [before], {len(operands): 0}
    return pl.pallas_call(
        join_kernel,
        grid=(count,),
        in_specs=specs,
        out_specs=[pl.BlockSpec((width, half), lambda s: (s + first, 0)), whole((8, LANES))],
        out_shape=[
            jax.ShapeDtypeStruct((valid, half), jnp.bfloat16), jax.ShapeDtypeStruct((8, LANES), jnp.float32),
        ],
        input_output_aliases=aliases,
        compiler_params=params(),
        cost_estimate=pl.CostEstimate(flops=height * half, bytes_accessed=6 * height * half, transcendentals=0),
        name="join",
    )(*operands)


def hidden_kernel(samples, count, chips, base_ref, _, *refs):
    part_refs, (b1_ref, w2_ref, w3_ref), refs = refs[:count], refs[count:count + 3], refs[count + 3:]
    residual_ref, kept_ref, sent_ref, *share_refs, first, second = refs
    rows = part_refs[0].shape[0] - 16
    coord, pts = base_ref[1], base_ref[2]
    total = sum(ref[...].astype(jnp.float32) for ref in part_refs)
    sums = jnp.sum(total[rows:rows + 3, :2 * LANES], axis=0, keepdims=True)
    row = lax.broadcasted_iota(jnp.int32, (rows, LANES), 0)
    lane = lax.broadcasted_iota(jnp.int32, (rows, LANES), 1)

    def choose(values, index):
        return jnp.sum(jnp.where(lane == index, values, 0.0), axis=1, keepdims=True)

    point = lax.div(row, samples)
    squares = choose(sums[:, :LANES], row + lax.rem(coord * rows, LANES))
    source = choose(sums[:, LANES:], point + coord * (rows // samples))
    one = jnp.tanh(total[:rows] + b1_ref[...]).astype(jnp.bfloat16)
    two = jnp.tanh(
        lax.dot_general(one, w2_ref[...], (((1,), (1,)), ((), ())), preferred_element_type=jnp.float32)
    ).astype(jnp.bfloat16).astype(jnp.float32)
    w3 = w3_ref[...]
    values = READOUT * jnp.sum(two * w3, axis=1, keepdims=True)
    stein = (squares - D) / (NOISE_SCALE * NOISE_SCALE * samples)
    terms = jnp.broadcast_to(stein * values, (rows, LANES))
    if rows < LANES:
        terms = jnp.concatenate([terms, jnp.zeros((LANES - rows, LANES), jnp.float32)], axis=0)
    terms = jnp.where(lax.div(lane, samples) == point, terms.T[:rows], 0.0)
    residual = jnp.sum(terms, axis=1, keepdims=True) - source
    for number in range(rows // samples):
        residual_ref[number:number + 1] = jnp.broadcast_to(residual[number * samples:number * samples + 1], (1, LANES))
    cotangent = residual * stein
    readout = READOUT * jnp.sum(cotangent * two, axis=0, keepdims=True)
    pre_two = (READOUT * cotangent * w3 * (1.0 - two * two)).astype(jnp.bfloat16)
    wide = one.astype(jnp.float32)
    pre_one = jnp.dot(pre_two, w2_ref[...], preferred_element_type=jnp.float32) * (1.0 - wide * wide)
    first[...] = pre_one.astype(jnp.bfloat16)
    bias = jnp.sum(first[...].astype(jnp.float32), axis=0, keepdims=True)
    share = first.shape[1] // (2 * chips)
    for by, ref in enumerate(share_refs):
        chip = lax.rem(lax.div(pts, 2) + by, chips)
        for half in range(2):
            index = chip * 2 + (pts + half) % 2
            ref[:, half * share:(half + 1) * share] = first[:, pl.ds(pl.multiple_of(index * share, share), share)]
    height, wide = kept_ref.shape[3] - 16, first.shape[1]
    outer = kept_ref.shape[2]
    second[:wide] = jnp.dot(pre_two.T, one, preferred_element_type=jnp.float32).astype(jnp.bfloat16)
    second[wide:] = jnp.concatenate([readout, bias, jnp.zeros((14, wide), jnp.float32)], axis=0).astype(jnp.bfloat16)
    for other_core, ref in enumerate((kept_ref, sent_ref)):
        for by in range(chips):
            index = lax.rem(lax.div(pts, 2) + by, chips) * 2 + (pts + other_core) % 2
            lanes = pl.ds(pl.multiple_of(index * share, share), share)
            for other in range(2):
                for shift in range(outer):
                    block = lax.rem(lax.div(coord, 2) + shift, outer) * 2 + (coord + other) % 2
                    rows_of = pl.ds(pl.multiple_of(block * height, height), height)
                    ref[by, other, shift, :height] = second[rows_of, lanes]
                    ref[by, other, shift, height:] = second[wide:, lanes]


def hidden_layers(base, after, parts, b1, w2, w3, samples, chips, blocks):
    rows, hidden = parts[0].shape[0] - 16, parts[0].shape[1]
    shapes = [(rows // samples, LANES)] + [(chips, 2, blocks // 2, hidden // blocks + 16, hidden // chips // 2)] * 2
    shapes += [(rows, hidden // chips)] * chips
    types = [jnp.float32] + [jnp.bfloat16] * (2 + chips)
    operands = [*parts, b1[None, :], w2, w3.astype(jnp.float32)[None, :]]
    return pl.pallas_call(
        functools.partial(hidden_kernel, samples, len(parts), chips),
        grid=(1,),
        in_specs=[pl.BlockSpec(memory_space=pltpu.SMEM), pl.BlockSpec(memory_space=pl.ANY)]
        + [whole(a.shape) for a in operands],
        out_specs=[whole(shape) for shape in shapes],
        out_shape=[jax.ShapeDtypeStruct(shape, kind) for shape, kind in zip(shapes, types)],
        scratch_shapes=[pltpu.VMEM((rows, hidden), jnp.bfloat16), pltpu.VMEM((hidden + 16, hidden), jnp.bfloat16)],
        compiler_params=params(),
        cost_estimate=pl.CostEstimate(
            flops=6 * rows * hidden * hidden, bytes_accessed=4 * hidden * hidden, transcendentals=2 * rows * hidden
        ),
        name="hidden",
    )(base, after, *operands)


def block_width(valid):
    tiles = -(-valid // LANES)
    best = min((8, 7, 6, 5), key=lambda t: -(-tiles // t) * t)
    return best * LANES


def shards(point_seed, pert_seed, source_coef, w1, b1, w2, w3):
    coord_count = lax.axis_size("coord")
    pts_count = lax.axis_size("pts")
    chips = pts_count // 2
    hidden, valid = w1.shape
    points_here, samples = pert_seed.shape
    rows_here = points_here * samples
    rows_local = rows_here // coord_count
    points_local = points_here // coord_count
    coord_index = lax.axis_index("coord")
    pts_index = lax.axis_index("pts")
    share = hidden // pts_count
    width = block_width(valid)
    steps = -(-valid // width)
    base = jnp.stack([coord_index * valid, coord_index, pts_index]).astype(jnp.int32)

    def shift(a, by):
        return jax.tree.map(
            lambda leaf: lax.ppermute(
                leaf, "pts", [(i, (i + 2 * by) % pts_count) for i in range(pts_count)]
            ), a,
        )

    other_seeds = [shift((pert_seed, point_seed), by) for by in range(1, chips)]

    pert, point = pert_seed.T, point_seed[None, :]
    own, near, far = forward(base, pert, point, source_coef[None, :], w1.T, width, coord_count)
    others_in = [(a.T, b[None, :]) for a, b in other_seeds]
    outer = coord_count // 2

    def across(a):
        return lax.ppermute(a, "coord", [(i, i ^ 1) for i in range(coord_count)])

    def along(a, by):
        return lax.ppermute(a, "coord", [(i, (i + 2 * by) % coord_count) for i in range(coord_count)])

    early = steps // 2 + (steps // 2) % 2
    cuts = [(0, early), (early, steps - early)]

    def redraws(number, after):
        first, count = cuts[number]
        held = [None] * len(others_in)
        for at, size in ((0, -(-count // 2)), (-(-count // 2), count // 2)):
            made = [
                redraw(base, a, b, after, z, width, first + at, size, first, count)
                for (a, b), z in zip(others_in, held)
            ]
            held = [z for z, _ in made]
            after = yield held, sum(mark for _, mark in made)

    draws = redraws(0, [near])
    _, mark = next(draws)
    parts = combine(near, across(far), mark)
    drawn_first, mark = draws.send([parts[0]])
    parts = [parts[0]] + [along(parts[by], by) for by in range(1, outer)]
    residual, kept, given, *sent = hidden_layers(base, mark, parts, b1, w2, w3, samples, chips, coord_count)
    residual = residual[:, 0]
    mine = jnp.concatenate([sent[0]] + [shift(sent[by], by) for by in range(1, chips)], axis=0)
    draws = redraws(1, [mine])
    _, mark = next(draws)
    if rows_local == LANES:
        cotangent = [mine] + [along(mine, by) for by in range(1, outer)] + [across(mine)]
        got, mark = stack(mark, *cotangent[1:outer])
        got = across(got)
        cotangent += [got[i] for i in range(outer - 1)]
        places = [(other, shift) for other in range(2) for shift in range(outer)]
        turn = base
    else:
        gathered = lax.all_gather(mine, "coord", axis=0)
        cotangent = [gathered[i] for i in range(coord_count)]
        turn = jnp.zeros_like(base)
    def add(own_part, *received):
        return sum((a.astype(jnp.float32) for a in received), own_part.astype(jnp.float32)).astype(jnp.bfloat16)

    swap = [(i, i ^ 1) for i in range(pts_count)]
    second = add(kept, lax.ppermute(given, "pts", swap))
    drawn_second, last_mark = draws.send([mark, second])
    drawn = [drawn_first, drawn_second]
    second = add(second[0], *[shift(second[by], by) for by in range(1, chips)])
    if rows_local != LANES:
        rows = jnp.stack(cotangent)[:, :chips * rows_local].reshape(coord_count, chips, rows_local, -1)
        rows = rows.transpose(1, 0, 2, 3).reshape(chips, -1, LANES, 2 * share).transpose(1, 0, 2, 3)
        rows = rows.reshape(-1, chips * LANES, 2 * share)
        cotangent = [rows[i] for i in range(rows.shape[0])]
        places = [(i % 2, -(i // 2) % (len(cotangent) // 2)) for i in range(len(cotangent))]

    def part(after, number, first, count, joined=None):
        keep, send, *out, mark = gradient(
            turn, after, cotangent, places, own, drawn[number], width, first, count, cuts[number][0], valid, joined
        )
        return mark[0, 0], keep, lax.ppermute(send, "pts", swap), *out

    mark, *one = part([second, last_mark], 0, *cuts[0])
    second = add(second[0], across(second[1]), mark)
    _, *two = part([second], 1, *cuts[1])

    def place(after, part, cut, out):
        (keep, got), (first, size) = part, cut
        wide = width * math.gcd(size, first, 2)
        out, mark = join(after, keep, got, out, wide, first * width // wide, valid)
        return out, mark[0, 0]

    out, mark = place([], one, cuts[0], None)
    second = add(second[0], *[along(second[by], by) for by in range(1, outer)], mark)
    out, mark = place([second], two, cuts[1], out)
    height = hidden // coord_count
    joined = jnp.zeros((second.shape[0], hidden), jnp.float32) + mark
    for by in range(pts_count):
        block = second if by == 0 else lax.ppermute(second, "pts", [(i, (i + by) % pts_count) for i in range(pts_count)])
        joined = lax.dynamic_update_slice_in_dim(
            joined, block.astype(jnp.float32), (pts_index - by) % pts_count * share, 1
        )
    readout, bias = (
        lax.dynamic_slice_in_dim(joined[row], coord_index * height, height, 0) for row in (height, height + 1)
    )
    second = joined[:height]

    return (residual, out.T, second, bias, readout)


def solution(mesh):
    return jax.shard_map(
        shards,
        mesh=mesh,
        in_specs=(P("pts"), P("pts", None), P("coord"), P(None, "coord"), P(), P(), P()),
        out_specs=(
            P(("pts", "coord")),
            P("pts", "coord"),
            P("coord", None),
            P("coord"),
            P("coord"),
        ),
        check_vma=False,
    )
```
